32 devices in a mesh: grp: 2 (over x), seq: 16 (over z, y, core).
Axes of the slice: x: 2, y: 2, z: 4, core: 2. Of those that a mesh axis runs over, the one named last changes fastest.
Arguments:
- out_grads: bfloat16 [4096, 8192], P(('grp', 'seq')), parts along dimension 0
- layer_inputs: bfloat16 [4096, 28672], P(('grp', 'seq')), parts along dimension 0
- factor_u: bfloat16 [64, 8192], P('seq'), may hold values from -0.0625 to 0.0625
- factor_v: bfloat16 [64, 28672], P('seq'), may hold values from -0.005859375 to 0.005859375
- seq_lengths: int32 [128], P('grp'), parts along dimension 0, may hold values from 1 to 125, as said below
Outputs:
- scores: float32 [2, 128], P(None, ('grp', 'seq')), parts along dimension 1
The draws below stay inside these ranges and needn't reach their ends.
There are 2 independent parts, one for each index of `grp`. The reference program is written for one: setup_inputs(seed, part) draws one part's arguments, and reference() takes and returns one part's arrays. A program takes and returns all parts, laid end to end along the dimension named above; an argument that names none is the same for every part. Nothing has to cross between parts.
Inputs may be any that keep to these rules, and one draw needn't show every extreme that they name: `seq_lengths`: entries b * 4 to (b + 1) * 4 - 1 are the lengths of the sequences in token-row block b, laid out in order from the block's first row. Each block's lengths sum to at most 128, which some block reaches in every draw; all lengths of a part sum to exactly 66 times the number of blocks.
All inputs are finite; a program needn't handle non-finite values.
Results may differ from the reference program's by a relative error of at most 0.0003.
Values may be sent and summed in bfloat16 or wider, within the bound.
No kernel may reach another device: no remote copies, remote signals or barrier semaphores. Data moves between devices by JAX's collectives and lax.ppermute only.
A program may use at most 128 MiB of HBM per device.

```python
import math
import jax
import jax.numpy as jnp
from jax import lax

D = 8192
FF = 28672
RANK = 32
SEQ_DEV = 4
LIVE_DEV = 66
TOK_CAP = 128
TOK_ROWS = 2048
SEQS = 64
FROWS = 64
QUERIES = 2
N_SEQ = 16


def scaled_rows(noise_field, key, shared, spread):
    key_common, key_rows, key_cols = jax.random.split(key, 3)
    row_total, col_total = noise_field.shape
    common = jax.random.normal(key_common, (col_total,), jnp.float32)
    log_spread = math.log(spread)
    row_scale = jnp.exp((jax.random.uniform(key_rows, (row_total, 1), jnp.float32) - 0.5) * log_spread)
    col_scale = jnp.exp((jax.random.uniform(key_cols, (1, col_total), jnp.float32) - 0.5) * log_spread)
    return (noise_field + shared * common[None, :]) * row_scale * col_scale


def draw_out_grads(key, part):
    key = jax.random.fold_in(key, 21)
    key_noise, key_rest = jax.random.split(key)
    noise_field = jax.random.normal(key_noise, (TOK_ROWS, D), jnp.float32)
    values = scaled_rows(noise_field, key_rest, 0.5, 10.0)
    return values.astype(jnp.bfloat16)


def draw_layer_inputs(key, part):
    key = jax.random.fold_in(key, 29)
    key_noise, key_rest = jax.random.split(key)
    noise_field = jax.random.normal(key_noise, (TOK_ROWS, FF), jnp.float32)
    values = scaled_rows(noise_field, key_rest, 0.5, 10.0)
    return values.astype(jnp.bfloat16)


def draw_seq_lengths(key, part):
    key = jax.random.fold_in(key, 37)
    key_order, key_level, key_weight = jax.random.split(key, 3)
    device_count = SEQS // SEQ_DEV
    device_order = jax.random.permutation(key_order, device_count)
    levels = jax.random.randint(key_level, (device_count,), 0, LIVE_DEV - SEQ_DEV + 1, jnp.int32)
    levels = levels.at[0].set(LIVE_DEV - SEQ_DEV).at[1].set(0).at[2 % device_count].set(LIVE_DEV - SEQ_DEV)
    totals_in_order = (LIVE_DEV + levels - jnp.roll(levels, -1)).astype(jnp.int32)
    totals = jnp.zeros((device_count,), jnp.int32).at[device_order].set(totals_in_order)
    weights = jax.random.randint(key_weight, (device_count, SEQ_DEV), 1, 64, jnp.int32)
    first_only = jnp.zeros((SEQ_DEV,), jnp.int32).at[0].set(1)
    weights = weights.at[device_order[0]].set(first_only)
    cumulative = jnp.cumsum(weights, axis=1).astype(jnp.int32)
    spare_rows = totals - SEQ_DEV
    cut_points = spare_rows[:, None] * cumulative // cumulative[:, -1:]
    previous = jnp.concatenate([jnp.zeros((device_count, 1), jnp.int32), cut_points[:, :-1]], axis=1)
    return (1 + cut_points - previous).reshape(-1).astype(jnp.int32)


def steps_of(rng, shape, cuts, low, top_value):
    level, own = 1.0, jax.random.fold_in(rng, 6)
    for dim, shards_of in cuts:
        draws = jnp.exp(jax.random.uniform(jax.random.fold_in(own, dim), (shards_of,), jnp.float32, low / len(cuts), top_value / len(cuts)))
        level = level * jnp.repeat(draws, shape[dim] // shards_of).reshape([-1 if axis == dim else 1 for axis in range(len(shape))])
    return level


def bell_draw(rng, dims, deviation, limit, pieces=(), held_as=jnp.bfloat16):
    array = jax.random.normal(rng, dims, jnp.float32) * deviation
    if len(pieces) > 0:
        array = steps_of(rng, dims, pieces, -0.22, 0.18) * array
    return jnp.clip(array, min=-limit, max=limit).astype(held_as)


def setup_inputs(seed: int = 0, part: int = 0) -> dict:
    key_of = jax.random.split(jax.random.key(seed), 6)
    part_keys = jax.random.split(jax.random.fold_in(key_of[5], part), 6)
    return {
        "out_grads": draw_out_grads(jax.random.fold_in(jax.random.fold_in(key_of[5], part), 71), part),
        "layer_inputs": draw_layer_inputs(jax.random.fold_in(jax.random.fold_in(key_of[5], part), 71), part),
        "factor_u": bell_draw(key_of[2], (FROWS, D), D ** -0.5, 0.0625, ((0, 16),)),
        "factor_v": bell_draw(key_of[3], (FROWS, FF), (FF * RANK) ** -0.5, 0.005859375, ((0, 16),)),
        "seq_lengths": draw_seq_lengths(jax.random.fold_in(jax.random.fold_in(key_of[5], part), 71), part),
    }


EPSILON = 1e-06

def sequence_rows(seq_lengths):
    length_table = seq_lengths.reshape(N_SEQ, SEQ_DEV).astype(jnp.int32)
    seq_ends = jnp.cumsum(length_table, axis=1).astype(jnp.int32)
    positions = jnp.arange(TOK_CAP, dtype=jnp.int32)
    return lax.optimization_barrier(jnp.sum((positions[None, :, None] >= seq_ends[:, None, :]).astype(jnp.int32), axis=2))

def block_norm(block_data):
    grad_rows, input_rows, local_seq = block_data
    gram_out = jnp.dot(grad_rows, grad_rows.T, preferred_element_type=jnp.float32)
    gram_in = jnp.dot(input_rows, input_rows.T, preferred_element_type=jnp.float32)
    member = (local_seq[:, None] == jnp.arange(SEQ_DEV, dtype=jnp.int32)[None, :]).astype(jnp.float32)
    return jnp.einsum('tk,tu,uk->k', member, gram_out * gram_in, member, precision=lax.Precision.HIGHEST)

def reference(out_grads, layer_inputs, factor_u, factor_v, seq_lengths):
    local_seq = sequence_rows(seq_lengths)
    proj_out = jnp.dot(out_grads, factor_u.T, preferred_element_type=jnp.float32)
    proj_in = jnp.dot(layer_inputs, factor_v.T, preferred_element_type=jnp.float32)
    token_score = lax.optimization_barrier(jnp.sum((proj_out * proj_in).reshape(TOK_ROWS, QUERIES, RANK), axis=2))
    member_all = (local_seq[:, :, None] == jnp.arange(SEQ_DEV, dtype=jnp.int32)[None, None, :]).astype(jnp.float32)
    numerator = jnp.einsum('btq,btk->qbk', token_score.reshape(N_SEQ, TOK_CAP, QUERIES), member_all, precision=lax.Precision.HIGHEST)
    numerator = numerator.reshape(QUERIES, SEQS)
    block_norms = lax.map(block_norm, (out_grads.reshape(N_SEQ, TOK_CAP, D), layer_inputs.reshape(N_SEQ, TOK_CAP, FF), local_seq))
    self_norm = block_norms.reshape(SEQS) / (D * FF)
    return numerator / jnp.sqrt(self_norm + EPSILON)[None, :]
```

```python
import functools

import jax
import jax.numpy as jnp
from jax import lax
from jax.experimental import pallas as pl
from jax.experimental.pallas import tpu as pltpu
from jax.sharding import PartitionSpec as P

RANK = 32
EPSILON = 1e-06
PACK = 16
VMEM_BYTES = 38 * 1024 * 1024

NT = (((1,), (1,)), ((), ()))


def inner_rows(left, right):
    return lax.dot_general(left, right, NT, preferred_element_type=jnp.float32)


def sequence_ends(lengths_ref, block, seq_dev):
    ends, total = [], 0
    for k in range(seq_dev):
        total = total + lengths_ref[block * seq_dev + k]
        ends.append(total)
    return ends


def in_sequence(positions, ends, k):
    low = 0 if k == 0 else ends[k - 1]
    return ((positions >= low) & (positions < ends[k])).astype(jnp.float32)


def norm_kernel(seq_dev, lengths_ref, out_ref, in_ref, norm_ref):
    tok_cap = out_ref.shape[0]
    width_out, width_in = out_ref.shape[1], in_ref.shape[1]
    gram_out = inner_rows(out_ref[...], out_ref[...])
    gram_in = inner_rows(in_ref[...], in_ref[...])
    paired = gram_out * gram_in
    ends = sequence_ends(lengths_ref, lax.axis_index("seq"), seq_dev)
    rows = lax.broadcasted_iota(jnp.int32, (tok_cap, 1), 0)
    cols = lax.broadcasted_iota(jnp.int32, (1, tok_cap), 1)
    lanes = lax.broadcasted_iota(jnp.int32, norm_ref.shape, 1)
    norms = jnp.zeros(norm_ref.shape, jnp.float32)
    for k in range(seq_dev):
        by_col = jnp.sum(paired * in_sequence(rows, ends, k), axis=0, keepdims=True)
        value = jnp.sum(by_col * in_sequence(cols, ends, k), axis=1, keepdims=True)
        norms = jnp.where(lanes == k, value / (width_out * width_in), norms)
    norm_ref[...] = norms


def score_kernel(seq_dev, rank_rows, by_xor, count, lengths_ref, norm_ref, out_ref, in_ref, *refs):
    block_refs, score_ref = refs[:count], refs[count]
    tok_cap = out_ref.shape[0]
    chunks = PACK // rank_rows
    wide_out, wide_in = out_ref.shape[1] // chunks, in_ref.shape[1] // chunks
    total = sum(ref.shape[0] for ref in block_refs)
    lanes = lax.broadcasted_iota(jnp.int32, (1, total), 1)
    lane_chunk = (lanes % PACK) // rank_rows

    def project(tokens_ref, wide, offset):
        held = jnp.zeros((tok_cap, total), jnp.float32)
        rows = jnp.concatenate([ref[:, offset : offset + wide] for ref in block_refs], axis=0)
        for j in range(chunks):
            part = inner_rows(tokens_ref[:, j * wide : (j + 1) * wide], rows)
            held = jnp.where(lane_chunk == j, part, held)
        summed = held
        for j in range(1, chunks):
            summed = summed + pltpu.roll(held, total - j * rank_rows, 1)
        return summed

    product = project(out_ref, wide_out, 0) * project(in_ref, wide_in, wide_out)
    me = lax.axis_index("seq")
    source = lanes // PACK
    if by_xor:
        source = source ^ me
    query = jnp.where(lane_chunk == 0, (source * rank_rows) // RANK, -1)
    ends = sequence_ends(lengths_ref, me, seq_dev)
    positions = lax.broadcasted_iota(jnp.int32, (tok_cap, 1), 0)
    at_query = lax.broadcasted_iota(jnp.int32, score_ref.shape, 0)
    at_seq = lax.broadcasted_iota(jnp.int32, score_ref.shape, 1)
    numerator = jnp.zeros(score_ref.shape, jnp.float32)
    for k in range(seq_dev):
        by_row = jnp.sum(product * in_sequence(positions, ends, k), axis=0, keepdims=True)
        for q in range(score_ref.shape[0]):
            value = jnp.sum(jnp.where(query == q, by_row, 0.0), axis=1, keepdims=True)
            numerator = jnp.where((at_query == q) & (at_seq == k), value, numerator)
    score_ref[...] = numerator / jnp.sqrt(norm_ref[0:1, 0:seq_dev] + EPSILON)


def gather_blocks(own, devices):
    if devices != 16:
        return False, [lax.all_gather(own, "seq", axis=0, tiled=True)]

    def swap(value, mask):
        return lax.ppermute(value, "seq", [(i, i ^ mask) for i in range(devices)])

    blocks = {0: own}
    blocks[2] = swap(own, 2)
    for z in (4, 8, 12):
        blocks[z] = swap(own, z)
    for z in (4, 8, 12):
        blocks[z + 2] = swap(blocks[z], 2)
    for b in list(blocks):
        blocks[b + 1] = swap(blocks[b], 1)
    return True, [blocks[b] for b in range(devices)]


def local(out_grads, layer_inputs, factor_u, factor_v, seq_lengths):
    devices = lax.axis_size("seq")
    seq_dev = seq_lengths.shape[0] // devices
    rank_rows = factor_u.shape[0]
    chunks = PACK // rank_rows
    queries = rank_rows * devices // RANK
    own = jnp.concatenate(
        [
            jnp.concatenate(jnp.split(factor_u, chunks, axis=1), axis=0),
            jnp.concatenate(jnp.split(factor_v, chunks, axis=1), axis=0),
        ],
        axis=1,
    )
    by_xor, blocks = gather_blocks(own, devices)
    smem = pl.BlockSpec(memory_space=pltpu.SMEM)
    vmem = pl.BlockSpec(memory_space=pltpu.VMEM)
    params = pltpu.CompilerParams(vmem_limit_bytes=VMEM_BYTES)
    tok_cap, width_out = out_grads.shape
    width = width_out + layer_inputs.shape[1]
    norms = pl.pallas_call(
        functools.partial(norm_kernel, seq_dev),
        out_shape=jax.ShapeDtypeStruct((8, 128), jnp.float32),
        in_specs=[smem, vmem, vmem],
        out_specs=vmem,
        compiler_params=params,
        cost_estimate=pl.CostEstimate(
            flops=2 * tok_cap * tok_cap * width, bytes_accessed=2 * tok_cap * width, transcendentals=0
        ),
    )(seq_lengths, out_grads, layer_inputs)
    total = sum(b.shape[0] for b in blocks)
    return pl.pallas_call(
        functools.partial(score_kernel, seq_dev, rank_rows, by_xor, len(blocks)),
        out_shape=jax.ShapeDtypeStruct((queries, seq_dev), jnp.float32),
        in_specs=[smem, vmem, vmem, vmem] + [vmem] * len(blocks),
        out_specs=vmem,
        compiler_params=params,
        cost_estimate=pl.CostEstimate(
            flops=2 * tok_cap * total * width, bytes_accessed=2 * tok_cap * width, transcendentals=0
        ),
    )(seq_lengths, norms, out_grads, layer_inputs, *blocks)


def solution(mesh):
    in_specs = (
        P(("grp", "seq"), None),
        P(("grp", "seq"), None),
        P("seq", None),
        P("seq", None),
        P("grp"),
    )
    out_specs = P(None, ("grp", "seq"))
    return jax.shard_map(local, mesh=mesh, in_specs=in_specs, out_specs=out_specs, check_vma=False)
```

```python
import functools

import jax
import jax.numpy as jnp
from jax import lax
from jax.experimental import pallas as pl
from jax.experimental.pallas import tpu as pltpu
from jax.sharding import PartitionSpec as P

RANK = 32
EPSILON = 1e-06
PACK = 16
TOKEN_PIECES = 8

NT = (((1,), (1,)), ((), ()))


def inner_rows(left, right):
    return lax.dot_general(left, right, NT, preferred_element_type=jnp.float32)


def sequence_ends(lengths_ref, block, seq_dev):
    ends, total = [], 0
    for k in range(seq_dev):
        total = total + lengths_ref[block * seq_dev + k]
        ends.append(total)
    return ends


def in_sequence(positions, ends, k):
    low = 0 if k == 0 else ends[k - 1]
    return ((positions >= low) & (positions < ends[k])).astype(jnp.float32)


def first_half(paired):
    return lax.axis_index("grp") % 2 if paired else 0


def turn(paired, chunks):
    return lax.axis_index("seq") % chunks if paired else 0


def pack_kernel(chunks, paired, u_ref, v_ref, both_ref, *own_refs):
    rank_rows = u_ref.shape[0]
    member = lax.axis_index("seq") % chunks
    wide_u, wide_v = u_ref.shape[1] // (2 * chunks), v_ref.shape[1] // (2 * chunks)
    for side in range(2):
        half = first_half(paired) ^ side
        place = 0
        for ref, wide in ((u_ref, wide_u), (v_ref, wide_v)):
            rows = []
            for g in range(chunks):
                start = pl.multiple_of(((g ^ member) * 2 + half) * wide, 128)
                rows.append(ref[:, pl.ds(start, wide)].astype(jnp.float32))
            piece = jnp.concatenate(rows, axis=0).astype(both_ref.dtype)
            both_ref[side * PACK : (side + 1) * PACK, place : place + wide] = piece
            if side == 0:
                for own_ref in own_refs:
                    own_ref[:, place : place + wide] = piece
            place += wide


def norm_kernel(seq_dev, lengths_ref, out_hbm, in_hbm, norm_ref, out_ref, in_ref, out_sem, in_sem):
    tok_cap = out_ref.shape[0]
    copies = []
    for piece in range(TOKEN_PIECES):
        for hbm, ref, sem in ((out_hbm, out_ref, out_sem), (in_hbm, in_ref, in_sem)):
            wide = ref.shape[1] // TOKEN_PIECES
            cols = pl.ds(piece * wide, wide)
            copy = pltpu.make_async_copy(hbm.at[:, cols], ref.at[:, cols], sem.at[piece])
            copy.start()
            copies.append((copy, ref, cols))
    grams = [jnp.zeros((tok_cap, tok_cap), jnp.float32) for _ in range(2)]
    for i, (copy, ref, cols) in enumerate(copies):
        copy.wait()
        tokens = ref[:, cols]
        grams[i % 2] = grams[i % 2] + inner_rows(tokens, tokens)
    paired = grams[0] * grams[1]
    ends = sequence_ends(lengths_ref, lax.axis_index("seq"), seq_dev)
    rows = lax.broadcasted_iota(jnp.int32, (tok_cap, 1), 0)
    cols = lax.broadcasted_iota(jnp.int32, (1, tok_cap), 1)
    lanes = lax.broadcasted_iota(jnp.int32, norm_ref.shape, 1)
    norms = jnp.zeros(norm_ref.shape, jnp.float32)
    for k in range(seq_dev):
        by_col = jnp.sum(paired * in_sequence(rows, ends, k), axis=0, keepdims=True)
        value = jnp.sum(by_col * in_sequence(cols, ends, k), axis=1, keepdims=True)
        norms = jnp.where(lanes == k, value / (out_ref.shape[1] * in_ref.shape[1]), norms)
    norm_ref[...] = norms


def swap_groups(value, bit, rank_rows):
    lanes = lax.broadcasted_iota(jnp.int32, (1, value.shape[1]), 1)
    shift = bit * rank_rows
    up = pltpu.roll(value, shift, 1)
    down = pltpu.roll(value, value.shape[1] - shift, 1)
    return jnp.where((lanes // shift) % 2 == 0, down, up)


def project(tokens_ref, half, offset, blocks, chunks, rank_rows, paired):
    wide = tokens_ref.shape[1] // (2 * chunks)
    sets = []
    for first in range(0, len(blocks), chunks):
        sets.append(
            [
                ref[row : row + PACK, offset : offset + wide]
                for ref, row in blocks[first : first + chunks]
            ]
        )
    group = lax.broadcasted_iota(jnp.int32, (PACK, wide), 0) // rank_rows
    result = None
    for j in range(chunks):
        rows = []
        for members in sets:
            merged = members[j]
            for g in range(1, chunks):
                merged = jnp.where(group == g, members[g ^ j], merged)
            rows.append(merged)
        rows = jnp.concatenate(rows, axis=0)
        start = pl.multiple_of(((j ^ turn(paired, chunks)) * 2 + half) * wide, 128)
        part = inner_rows(tokens_ref[:, pl.ds(start, wide)], rows)
        bit = 1
        while bit < chunks:
            if j & bit:
                part = swap_groups(part, bit, rank_rows)
            bit *= 2
        result = part if result is None else result + part
    return result


def both_projections(out_ref, in_ref, half, blocks, rank_rows, paired):
    chunks = PACK // rank_rows
    wide_out = out_ref.shape[1] // (2 * chunks)
    return (
        project(out_ref, half, 0, blocks, chunks, rank_rows, paired),
        project(in_ref, half, wide_out, blocks, chunks, rank_rows, paired),
    )


def partial_kernel(rank_rows, paired, rows, out_ref, in_ref, *refs):
    blocks = [(ref, row) for ref, row in zip(refs, rows)]
    held_ref = refs[len(rows)]
    held_out, held_in = both_projections(
        out_ref, in_ref, first_half(paired), blocks, rank_rows, paired
    )
    held_ref[0] = held_out
    held_ref[1] = held_in


def score_kernel(seq_dev, rank_rows, paired, rows, lengths_ref, norm_ref, held_ref, out_ref, in_ref, *refs):
    blocks = [(ref, row) for ref, row in zip(refs, rows)]
    score_ref = refs[len(rows)]
    tok_cap = out_ref.shape[0]
    held_out, held_in = both_projections(
        out_ref, in_ref, 1 - first_half(paired), blocks, rank_rows, paired
    )
    product = (held_ref[0] + held_out) * (held_ref[1] + held_in)
    me = lax.axis_index("seq")
    lanes = lax.broadcasted_iota(jnp.int32, (1, product.shape[1]), 1)
    source = lanes // rank_rows
    if paired:
        source = source ^ me
    query = (source * rank_rows) // RANK
    ends = sequence_ends(lengths_ref, me, seq_dev)
    positions = lax.broadcasted_iota(jnp.int32, (tok_cap, 1), 0)
    at_query = lax.broadcasted_iota(jnp.int32, score_ref.shape, 0)
    at_seq = lax.broadcasted_iota(jnp.int32, score_ref.shape, 1)
    numerator = jnp.zeros(score_ref.shape, jnp.float32)
    for k in range(seq_dev):
        by_row = jnp.sum(product * in_sequence(positions, ends, k), axis=0, keepdims=True)
        for q in range(score_ref.shape[0]):
            value = jnp.sum(jnp.where(query == q, by_row, 0.0), axis=1, keepdims=True)
            numerator = jnp.where((at_query == q) & (at_seq == k), value, numerator)
    score_ref[...] = numerator / jnp.sqrt(norm_ref[0:1, 0:seq_dev] + EPSILON)


def gather_blocks(both, own, devices):
    def swap(value, mask):
        return lax.ppermute(value, "seq", [(i, i ^ mask) for i in range(devices)])

    def across(value):
        return lax.ppermute(value, "grp", [(0, 1), (1, 0)])

    mine, other = {}, {}
    mine[4] = swap(own, 4)
    mine[8] = swap(own, 8)
    pair_y = swap(both, 2)
    own, mine[4] = lax.optimization_barrier((own, mine[4]))
    mine[12] = swap(own, 12)
    for z in (4, 8, 12):
        other[z] = across(mine[z])
        mine[z + 2] = swap(mine[z], 2)
        other[z + 2] = across(mine[z + 2])
    for held in (mine, other):
        for b in list(held):
            held[b + 1] = swap(held[b], 1)
    for b, value in ((0, both), (2, pair_y)):
        core = swap(value, 1)
        mine[b], other[b] = (value, 0), (value, PACK)
        mine[b + 1], other[b + 1] = (core, 0), (core, PACK)
    plain = lambda item: item if isinstance(item, tuple) else (item, 0)
    return [[plain(held[b]) for b in range(devices)] for held in (mine, other)]


def local(out_grads, layer_inputs, factor_u, factor_v, seq_lengths):
    devices = lax.axis_size("seq")
    paired = devices == 16 and lax.axis_size("grp") == 2
    seq_dev = seq_lengths.shape[0] // devices
    rank_rows = factor_u.shape[0]
    chunks = PACK // rank_rows
    queries = rank_rows * devices // RANK
    tok_cap, width_out = out_grads.shape
    width_in = layer_inputs.shape[1]
    width = width_out + width_in
    smem = pl.BlockSpec(memory_space=pltpu.SMEM)
    vmem = pl.BlockSpec(memory_space=pltpu.VMEM)
    hbm = pl.BlockSpec(memory_space=pl.ANY)
    params = pltpu.CompilerParams(vmem_limit_bytes=24 * 1024 * 1024)

    half_width = width // (2 * chunks)
    packed = pl.pallas_call(
        functools.partial(pack_kernel, chunks, paired),
        out_shape=[jax.ShapeDtypeStruct((2 * PACK, half_width), factor_u.dtype)]
        + [jax.ShapeDtypeStruct((PACK, half_width), factor_u.dtype)] * paired,
        in_specs=[vmem, vmem],
        out_specs=[vmem] * (1 + paired),
        compiler_params=params,
    )(factor_u, factor_v)
    if paired:
        mine, other = gather_blocks(packed[0], packed[1], devices)
    else:
        gathered = lax.all_gather(packed[0], "seq", axis=0, tiled=True)
        mine = [(gathered, 2 * PACK * b) for b in range(devices)]
        other = [(gathered, 2 * PACK * b + PACK) for b in range(devices)]

    norms, out_held, in_held = pl.pallas_call(
        functools.partial(norm_kernel, seq_dev),
        out_shape=[
            jax.ShapeDtypeStruct((8, 128), jnp.float32),
            jax.ShapeDtypeStruct(out_grads.shape, out_grads.dtype),
            jax.ShapeDtypeStruct(layer_inputs.shape, layer_inputs.dtype),
        ],
        in_specs=[smem, hbm, hbm],
        out_specs=[vmem] * 3,
        scratch_shapes=[pltpu.SemaphoreType.DMA((TOKEN_PIECES,))] * 2,
        compiler_params=params,
        cost_estimate=pl.CostEstimate(
            flops=2 * tok_cap * tok_cap * width, bytes_accessed=2 * tok_cap * width, transcendentals=0
        ),
    )(seq_lengths, out_grads, layer_inputs)

    frows = devices * rank_rows
    cost = pl.CostEstimate(
        flops=tok_cap * frows * width, bytes_accessed=(tok_cap + frows) * width, transcendentals=0
    )

    def refs_of(blocks):
        return [vmem] * len(blocks), [a for a, _ in blocks], tuple(row for _, row in blocks)

    specs, arrays, rows = refs_of(mine)
    held = pl.pallas_call(
        functools.partial(partial_kernel, rank_rows, paired, rows),
        out_shape=jax.ShapeDtypeStruct((2, tok_cap, frows), jnp.float32),
        in_specs=[vmem, vmem] + specs,
        out_specs=vmem,
        compiler_params=params,
        cost_estimate=cost,
    )(out_held, in_held, *arrays)
    specs, arrays, rows = refs_of(other)
    return pl.pallas_call(
        functools.partial(score_kernel, seq_dev, rank_rows, paired, rows),
        out_shape=jax.ShapeDtypeStruct((queries, seq_dev), jnp.float32),
        in_specs=[smem, vmem, vmem, vmem, vmem] + specs,
        out_specs=vmem,
        compiler_params=params,
        cost_estimate=cost,
    )(seq_lengths, norms, held, out_held, in_held, *arrays)


def solution(mesh):
    in_specs = (
        P(("grp", "seq"), None),
        P(("grp", "seq"), None),
        P("seq", None),
        P("seq", None),
        P("grp"),
    )
    out_specs = P(None, ("grp", "seq"))
    return jax.shard_map(local, mesh=mesh, in_specs=in_specs, out_specs=out_specs, check_vma=False)
```

```python
import functools

import jax
import jax.numpy as jnp
from jax import lax
from jax.experimental import pallas as pl
from jax.experimental.pallas import tpu as pltpu
from jax.sharding import PartitionSpec as P

RANK = 32
EPSILON = 1e-06
PACK = 16
SCORE_VMEM = 24 * 1024 * 1024
PACK_VMEM = 58 * 1024 * 1024

NT = (((1,), (1,)), ((), ()))


def inner_rows(left, right):
    return lax.dot_general(left, right, NT, preferred_element_type=jnp.float32)


def sequence_ends(lengths_ref, block, seq_dev):
    ends, total = [], 0
    for k in range(seq_dev):
        total = total + lengths_ref[block * seq_dev + k]
        ends.append(total)
    return ends


def in_sequence(positions, ends, k):
    low = 0 if k == 0 else ends[k - 1]
    return ((positions >= low) & (positions < ends[k])).astype(jnp.float32)


def first_half(paired):
    return lax.axis_index("grp") % 2 if paired else 0


def turn(paired, chunks):
    return lax.axis_index("seq") % chunks if paired else 0


def pack_kernel(chunks, paired, u_hbm, v_hbm, both_ref, *refs):
    *own_refs, u_ref, v_ref, sems = refs
    copies = [
        pltpu.make_async_copy(u_hbm, u_ref, sems.at[0]),
        pltpu.make_async_copy(v_hbm, v_ref, sems.at[1]),
    ]
    for copy in copies:
        copy.start()
    for copy in copies:
        copy.wait()
    rank_rows = u_ref.shape[0]
    member = lax.axis_index("seq") % chunks
    wide_u, wide_v = u_ref.shape[1] // (2 * chunks), v_ref.shape[1] // (2 * chunks)
    for side in range(2):
        half = first_half(paired) ^ side
        place = 0
        for ref, wide in ((u_ref, wide_u), (v_ref, wide_v)):
            rows = []
            for g in range(chunks):
                start = pl.multiple_of(((g ^ member) * 2 + half) * wide, 128)
                rows.append(ref[:, pl.ds(start, wide)].astype(jnp.float32))
            piece = jnp.concatenate(rows, axis=0).astype(both_ref.dtype)
            both_ref[side * PACK : (side + 1) * PACK, place : place + wide] = piece
            if side == 0:
                for own_ref in own_refs:
                    own_ref[:, place : place + wide] = piece
            place += wide


def norm_kernel(seq_dev, lengths_ref, out_ref, in_ref, norm_ref):
    tok_cap = out_ref.shape[0]
    gram_out = inner_rows(out_ref[...], out_ref[...])
    paired = gram_out * inner_rows(in_ref[...], in_ref[...])
    ends = sequence_ends(lengths_ref, lax.axis_index("seq"), seq_dev)
    rows = lax.broadcasted_iota(jnp.int32, (tok_cap, 1), 0)
    cols = lax.broadcasted_iota(jnp.int32, (1, tok_cap), 1)
    lanes = lax.broadcasted_iota(jnp.int32, norm_ref.shape, 1)
    norms = jnp.zeros(norm_ref.shape, jnp.float32)
    for k in range(seq_dev):
        by_col = jnp.sum(paired * in_sequence(rows, ends, k), axis=0, keepdims=True)
        value = jnp.sum(by_col * in_sequence(cols, ends, k), axis=1, keepdims=True)
        norms = jnp.where(lanes == k, value / (out_ref.shape[1] * in_ref.shape[1]), norms)
    norm_ref[...] = norms


def swap_groups(value, bit, rank_rows):
    lanes = lax.broadcasted_iota(jnp.int32, (1, value.shape[1]), 1)
    shift = bit * rank_rows
    up = pltpu.roll(value, shift, 1)
    down = pltpu.roll(value, value.shape[1] - shift, 1)
    return jnp.where((lanes // shift) % 2 == 0, down, up)


def merged_rows(blocks, offset, wide, j, chunks, rank_rows):
    group = lax.broadcasted_iota(jnp.int32, (PACK, wide), 0) // rank_rows
    rows = []
    for first in range(0, len(blocks), chunks):
        merged = None
        for g in range(chunks):
            ref, row = blocks[first + (g ^ j)]
            piece = ref[row : row + PACK, offset : offset + wide]
            merged = piece if merged is None else jnp.where(group == g, piece, merged)
        rows.append(merged)
    return jnp.concatenate(rows, axis=0)


def both_projections(out_ref, in_ref, half, blocks, rank_rows, paired):
    chunks = PACK // rank_rows
    results, offset = [], 0
    for ref in (out_ref, in_ref):
        wide = ref.shape[1] // (2 * chunks)
        result = None
        for j in range(chunks):
            rows = merged_rows(blocks, offset, wide, j, chunks, rank_rows)
            start = pl.multiple_of(((j ^ turn(paired, chunks)) * 2 + half) * wide, 128)
            part = inner_rows(ref[:, pl.ds(start, wide)], rows)
            bit = 1
            while bit < chunks:
                if j & bit:
                    part = swap_groups(part, bit, rank_rows)
                bit *= 2
            result = part if result is None else result + part
        results.append(result)
        offset += wide
    return results


def partial_kernel(rank_rows, paired, places, out_ref, in_ref, *refs):
    *array_refs, held_ref = refs
    blocks = [(array_refs[i], row) for i, row in places]
    half = first_half(paired)
    held_out, held_in = both_projections(
        out_ref, in_ref, half, blocks, rank_rows, paired
    )
    held_ref[0] = held_out
    held_ref[1] = held_in


def score_kernel(seq_dev, rank_rows, paired, places, lengths_ref, norm_ref, held_ref, out_ref, in_ref, *refs):
    *array_refs, score_ref = refs
    blocks = [(array_refs[i], row) for i, row in places]
    tok_cap = out_ref.shape[0]
    half = 1 - first_half(paired)
    held_out, held_in = both_projections(
        out_ref, in_ref, half, blocks, rank_rows, paired
    )
    product = (held_ref[0] + held_out) * (held_ref[1] + held_in)
    me = lax.axis_index("seq")
    lanes = lax.broadcasted_iota(jnp.int32, (1, product.shape[1]), 1)
    source = lanes // rank_rows
    if paired:
        source = source ^ me
    query = (source * rank_rows) // RANK
    ends = sequence_ends(lengths_ref, me, seq_dev)
    positions = lax.broadcasted_iota(jnp.int32, (tok_cap, 1), 0)
    at_query = lax.broadcasted_iota(jnp.int32, score_ref.shape, 0)
    at_seq = lax.broadcasted_iota(jnp.int32, score_ref.shape, 1)
    numerator = jnp.zeros(score_ref.shape, jnp.float32)
    for k in range(seq_dev):
        by_row = jnp.sum(product * in_sequence(positions, ends, k), axis=0, keepdims=True)
        for q in range(score_ref.shape[0]):
            value = jnp.sum(jnp.where(query == q, by_row, 0.0), axis=1, keepdims=True)
            numerator = jnp.where((at_query == q) & (at_seq == k), value, numerator)
    score_ref[...] = numerator / jnp.sqrt(norm_ref[0:1, 0:seq_dev] + EPSILON)


def after(value, *others):
    return lax.optimization_barrier((value, *others))[0]


def gather_blocks(both, own, devices, norm_step, lengths):
    def swap(value, mask):
        return lax.ppermute(value, "seq", [(i, i ^ mask) for i in range(devices)])

    def across(value):
        return lax.ppermute(value, "grp", [(0, 1), (1, 0)])

    def swap_core(values):
        group = jnp.concatenate(values, axis=0) if len(values) > 1 else values[0]
        return group, swap(group, 1)

    z1, z2, y0 = swap(own, 4), swap(own, 8), swap(both, 2)
    x1, y1, z3 = across(z1), swap(z1, 2), swap(after(own, z1), 12)
    z2 = after(z2, x1, y0)
    x2, y2 = across(z2), swap(z2, 2)
    xy1 = across(y1)
    first, first_core = swap_core([both, y0, z1, x1, y1, z2])
    z3 = after(z3, x2, first_core)
    x3, y3 = across(z3), swap(z3, 2)
    y2 = after(y2, xy1)
    xy2 = across(y2)
    second, second_core = swap_core([x2, y2, xy1, z3])
    y3 = after(y3, second_core)
    xy3 = across(y3)
    normed = norm_step(after(lengths, y3))
    third, third_core = swap_core([x3, y3, xy2])
    xy3 = after(xy3, normed)
    last, last_core = swap_core([xy3])
    mine, other = {}, {}
    spots = (
        (first, first_core, ((mine, 0), (other, 0), (mine, 2), (other, 2), (mine, 4), (other, 4), (mine, 6), (mine, 8))),
        (second, second_core, ((other, 8), (mine, 10), (other, 6), (mine, 12))),
        (third, third_core, ((other, 12), (mine, 14), (other, 10))),
        (last, last_core, ((other, 14),)),
    )
    for here, core, places in spots:
        for i, (held, b) in enumerate(places):
            held[b], held[b + 1] = (here, i * PACK), (core, i * PACK)
    return [mine[b] for b in range(devices)], [other[b] for b in range(devices)], normed


def refs_of(blocks):
    arrays, places = [], []
    for value, row in blocks:
        seen = [i for i, array in enumerate(arrays) if array is value]
        if not seen:
            arrays.append(value)
        places.append((seen[0] if seen else len(arrays) - 1, row))
    return arrays, tuple(places)


def local(out_grads, layer_inputs, factor_u, factor_v, seq_lengths):
    devices = lax.axis_size("seq")
    paired = devices == 16 and lax.axis_size("grp") == 2
    seq_dev = seq_lengths.shape[0] // devices
    rank_rows = factor_u.shape[0]
    chunks = PACK // rank_rows
    queries = rank_rows * devices // RANK
    tok_cap, width_out = out_grads.shape
    width_in = layer_inputs.shape[1]
    width = width_out + width_in
    smem = pl.BlockSpec(memory_space=pltpu.SMEM)
    vmem = pl.BlockSpec(memory_space=pltpu.VMEM)
    hbm = pl.BlockSpec(memory_space=pltpu.HBM)

    score_params = pltpu.CompilerParams(vmem_limit_bytes=SCORE_VMEM)
    half_width = width // (2 * chunks)
    packed = pl.pallas_call(
        functools.partial(pack_kernel, chunks, paired),
        out_shape=[jax.ShapeDtypeStruct((2 * PACK, half_width), factor_u.dtype)]
        + [jax.ShapeDtypeStruct((PACK, half_width), factor_u.dtype)] * paired,
        in_specs=[hbm, hbm],
        out_specs=[vmem] * (1 + paired),
        scratch_shapes=[
            pltpu.VMEM(factor_u.shape, factor_u.dtype),
            pltpu.VMEM(factor_v.shape, factor_v.dtype),
            pltpu.SemaphoreType.DMA((2,)),
        ],
        compiler_params=pltpu.CompilerParams(vmem_limit_bytes=PACK_VMEM),
    )(factor_u, factor_v)
    def norm_step(lengths):
        return pl.pallas_call(
            functools.partial(norm_kernel, seq_dev),
            out_shape=jax.ShapeDtypeStruct((8, 128), jnp.float32),
            in_specs=[smem, vmem, vmem],
            out_specs=vmem,
            compiler_params=score_params,
            cost_estimate=pl.CostEstimate(
                flops=2 * tok_cap * tok_cap * width,
                bytes_accessed=2 * tok_cap * width,
                transcendentals=0,
            ),
        )(lengths, out_grads, layer_inputs)

    if paired:
        mine, other, normed = gather_blocks(packed[0], packed[1], devices, norm_step, seq_lengths)
    else:
        normed = norm_step(seq_lengths)
        gathered = lax.all_gather(packed[0], "seq", axis=0, tiled=True)
        mine = [(gathered, 2 * PACK * b) for b in range(devices)]
        other = [(gathered, 2 * PACK * b + PACK) for b in range(devices)]

    frows = devices * rank_rows
    cost = pl.CostEstimate(
        flops=tok_cap * frows * width, bytes_accessed=(tok_cap + frows) * width, transcendentals=0
    )

    arrays, places = refs_of(mine)
    held = pl.pallas_call(
        functools.partial(partial_kernel, rank_rows, paired, places),
        out_shape=jax.ShapeDtypeStruct((2, tok_cap, frows), jnp.float32),
        in_specs=[vmem, vmem] + [vmem] * len(arrays),
        out_specs=vmem,
        compiler_params=score_params,
        cost_estimate=cost,
    )(out_grads, layer_inputs, *arrays)
    arrays, places = refs_of(other)
    return pl.pallas_call(
        functools.partial(score_kernel, seq_dev, rank_rows, paired, places),
        out_shape=jax.ShapeDtypeStruct((queries, seq_dev), jnp.float32),
        in_specs=[smem, vmem, vmem, vmem, vmem] + [vmem] * len(arrays),
        out_specs=vmem,
        compiler_params=score_params,
        cost_estimate=cost,
    )(seq_lengths, normed, held, out_grads, layer_inputs, *arrays)


def solution(mesh):
    in_specs = (
        P(("grp", "seq"), None),
        P(("grp", "seq"), None),
        P("seq", None),
        P("seq", None),
        P("grp"),
    )
    out_specs = P(None, ("grp", "seq"))
    return jax.shard_map(local, mesh=mesh, in_specs=in_specs, out_specs=out_specs, check_vma=False)
```

```python
import functools

import jax
import jax.numpy as jnp
from jax import lax
from jax.experimental import pallas as pl
from jax.experimental.pallas import tpu as pltpu
from jax.sharding import PartitionSpec as P

RANK = 32
EPSILON = 1e-06
PACK = 16
HEAD = 8192
SCORE_VMEM = 24 * 1024 * 1024
PACK_VMEM = 58 * 1024 * 1024

NT = (((1,), (1,)), ((), ()))


def inner_rows(left, right):
    return lax.dot_general(left, right, NT, preferred_element_type=jnp.float32)


def first_half(paired):
    return lax.axis_index("grp") % 2 if paired else 0


def turn(paired, chunks):
    return lax.axis_index("seq") % chunks if paired else 0


def pack_kernel(chunks, paired, u_hbm, v_hbm, both_ref, *refs):
    *own_refs, u_ref, v_ref, sems = refs
    copies = []
    for i, (hbm, ref) in enumerate(((u_hbm, u_ref), (v_hbm, v_ref))):
        wide = ref.shape[1] // chunks
        for j in range(chunks):
            cols = pl.ds(j * wide, wide)
            copies.append(pltpu.make_async_copy(hbm.at[:, cols], ref.at[:, cols], sems.at[i, j]))
    for copy in copies:
        copy.start()
    for copy in copies:
        copy.wait()
    rank_rows = u_ref.shape[0]
    member = lax.axis_index("seq") % chunks
    wide_u, wide_v = u_ref.shape[1] // (2 * chunks), v_ref.shape[1] // (2 * chunks)
    for side in range(2):
        half = first_half(paired) ^ side
        place = 0
        for ref, wide in ((u_ref, wide_u), (v_ref, wide_v)):
            rows = []
            for g in range(chunks):
                start = pl.multiple_of(((g ^ member) * 2 + half) * wide, 128)
                rows.append(ref[:, pl.ds(start, wide)].astype(jnp.float32))
            piece = jnp.concatenate(rows, axis=0).astype(both_ref.dtype)
            both_ref[side * PACK : (side + 1) * PACK, place : place + wide] = piece
            if side == 0:
                for own_ref in own_refs:
                    own_ref[:, place : place + wide] = piece
            place += wide


def head_kernel(after_ref, in_ref, gram_ref):
    head = in_ref[:, :HEAD]
    gram_ref[...] = inner_rows(head, head)


def norm_kernel(seq_dev, lengths_hbm, head_ref, out_ref, in_ref, norm_ref, member_ref, lengths_ref, sem):
    copy = pltpu.make_async_copy(lengths_hbm, lengths_ref, sem)
    copy.start()
    gram_out = inner_rows(out_ref[...], out_ref[...])
    tail = in_ref[:, HEAD:]
    paired = gram_out * (head_ref[...] + inner_rows(tail, tail))
    copy.wait()
    seqs, tok_cap = member_ref.shape
    which = lax.broadcasted_iota(jnp.int32, (seqs, tok_cap), 0)
    position = lax.broadcasted_iota(jnp.int32, (seqs, tok_cap), 1)
    block = lax.axis_index("seq")
    member = jnp.zeros((seqs, tok_cap), jnp.float32)
    low = 0
    for k in range(seq_dev):
        high = low + lengths_ref[block * seq_dev + k]
        inside = (which == k) & (position >= low) & (position < high)
        member = jnp.where(inside, 1.0, member)
        low = high
    member_ref[...] = member
    sums = jnp.dot(
        member, paired, precision=lax.Precision.HIGHEST, preferred_element_type=jnp.float32
    )
    value = jnp.sum(sums * member, axis=1, keepdims=True) / (out_ref.shape[1] * in_ref.shape[1])
    norm_ref[...] = jnp.sum(jnp.where(which == position, value, 0.0), axis=0, keepdims=True)


def swap_groups(value, bit, rank_rows):
    lanes = lax.broadcasted_iota(jnp.int32, (1, value.shape[1]), 1)
    shift = bit * rank_rows
    up = pltpu.roll(value, shift, 1)
    down = pltpu.roll(value, value.shape[1] - shift, 1)
    return jnp.where((lanes // shift) % 2 == 0, down, up)


def merged_rows(blocks, offset, wide, j, chunks, rank_rows):
    group = lax.broadcasted_iota(jnp.int32, (PACK, wide), 0) // rank_rows
    rows = []
    for first in range(0, len(blocks), chunks):
        merged = None
        for g in range(chunks):
            ref, row = blocks[first + (g ^ j)]
            piece = ref[row : row + PACK, offset : offset + wide]
            merged = piece if merged is None else jnp.where(group == g, piece, merged)
        rows.append(merged)
    return jnp.concatenate(rows, axis=0)


def both_projections(out_ref, in_ref, half, blocks, rank_rows, paired):
    chunks = PACK // rank_rows
    results, offset = [], 0
    for ref in (out_ref, in_ref):
        wide = ref.shape[1] // (2 * chunks)
        result = None
        for j in range(chunks):
            rows = merged_rows(blocks, offset, wide, j, chunks, rank_rows)
            start = pl.multiple_of(((j ^ turn(paired, chunks)) * 2 + half) * wide, 128)
            part = inner_rows(ref[:, pl.ds(start, wide)], rows)
            bit = 1
            while bit < chunks:
                if j & bit:
                    part = swap_groups(part, bit, rank_rows)
                bit *= 2
            result = part if result is None else result + part
        results.append(result)
        offset += wide
    return results


def partial_kernel(rank_rows, paired, places, out_ref, in_ref, *refs):
    *array_refs, held_ref = refs
    blocks = [(array_refs[i], row) for i, row in places]
    half = first_half(paired)
    held_out, held_in = both_projections(
        out_ref, in_ref, half, blocks, rank_rows, paired
    )
    held_ref[0] = held_out
    held_ref[1] = held_in


def score_kernel(rank_rows, paired, places, norm_ref, member_ref, held_ref, out_ref, in_ref, *refs):
    *array_refs, score_ref = refs
    blocks = [(array_refs[i], row) for i, row in places]
    half = 1 - first_half(paired)
    held_out, held_in = both_projections(
        out_ref, in_ref, half, blocks, rank_rows, paired
    )
    product = (held_ref[0] + held_out) * (held_ref[1] + held_in)
    me = lax.axis_index("seq")
    lanes = lax.broadcasted_iota(jnp.int32, (1, product.shape[1]), 1)
    source = lanes // rank_rows
    if paired:
        source = source ^ me
    query = (source * rank_rows) // RANK
    sums = jnp.dot(
        member_ref[...], product, precision=lax.Precision.HIGHEST, preferred_element_type=jnp.float32
    )
    seqs, tok_cap = member_ref.shape
    diagonal = lax.broadcasted_iota(jnp.int32, (seqs, tok_cap), 0) == lax.broadcasted_iota(
        jnp.int32, (seqs, tok_cap), 1
    )
    scale = jnp.sqrt(norm_ref[...] + EPSILON)
    for q in range(score_ref.shape[0]):
        value = jnp.sum(jnp.where(query == q, sums, 0.0), axis=1, keepdims=True)
        row = jnp.sum(jnp.where(diagonal, value, 0.0), axis=0, keepdims=True) / scale
        score_ref[q : q + 1, :] = row[:, : score_ref.shape[1]]


def gather_blocks(both, own, devices, lengths, head_step, norm_step, partial_step):
    def swap(value, mask):
        return lax.ppermute(value, "seq", [(i, i ^ mask) for i in range(devices)])

    def across(value):
        return lax.ppermute(value, "grp", [(0, 1), (1, 0)])

    gate = lambda *values: lax.optimization_barrier(values)
    stack = lambda *values: jnp.concatenate(values, axis=0)
    z1, z2, y0, both_core = swap(own, 4), swap(own, 8), swap(both, 2), swap(both, 1)
    z1, both_core, own = gate(z1, both_core, own)
    x1, y1, z3 = across(z1), swap(z1, 2), swap(own, 12)
    z2, x1, y1, y0, lengths = gate(z2, x1, y1, y0, lengths)
    x_near, y2 = across(stack(z2, y1)), swap(z2, 2)
    head = head_step(lengths)
    z3, y2, x_near, head, lengths = gate(z3, y2, x_near, head, lengths)
    x_far, y3 = across(stack(z3, y2)), swap(z3, 2)
    early = stack(y0, z1, y1, z2, x1)
    early_core = swap(early, 1)
    normed = norm_step(lengths, head)
    y3, norms = gate(y3, normed[0])
    x_last = across(y3)
    middle = stack(y2, z3, y3, x_near)
    middle_core = swap(middle, 1)
    mine, other = {}, {}

    def place(group, core, places):
        for i, (held, b) in enumerate(places):
            held[b], held[b + 1] = (group, i * PACK), (core, i * PACK)

    place(both, both_core, ((mine, 0), (other, 0)))
    place(early, early_core, ((mine, 2), (other, 2), (mine, 4), (mine, 6), (mine, 8), (other, 4)))
    place(middle, middle_core, ((mine, 10), (mine, 12), (mine, 14), (other, 8), (other, 6)))
    partial = partial_step([mine[b] for b in range(devices)])
    x_far, x_last, partial = gate(x_far, x_last, partial)
    late = stack(x_far, x_last)
    place(late, swap(late, 1), ((other, 12), (other, 10), (other, 14)))
    return [other[b] for b in range(devices)], (norms, normed[1]), partial


def refs_of(blocks):
    arrays, places = [], []
    for value, row in blocks:
        seen = [i for i, array in enumerate(arrays) if array is value]
        if not seen:
            arrays.append(value)
        places.append((seen[0] if seen else len(arrays) - 1, row))
    return arrays, tuple(places)


def local(out_grads, layer_inputs, factor_u, factor_v, seq_lengths):
    devices = lax.axis_size("seq")
    paired = devices == 16 and lax.axis_size("grp") == 2
    seq_dev = seq_lengths.shape[0] // devices
    rank_rows = factor_u.shape[0]
    chunks = PACK // rank_rows
    queries = rank_rows * devices // RANK
    tok_cap, width_out = out_grads.shape
    width_in = layer_inputs.shape[1]
    width = width_out + width_in
    vmem = pl.BlockSpec(memory_space=pltpu.VMEM)
    hbm = pl.BlockSpec(memory_space=pltpu.HBM)

    score_params = pltpu.CompilerParams(vmem_limit_bytes=SCORE_VMEM)
    half_width = width // (2 * chunks)
    packed = pl.pallas_call(
        functools.partial(pack_kernel, chunks, paired),
        out_shape=[jax.ShapeDtypeStruct((2 * PACK, half_width), factor_u.dtype)]
        + [jax.ShapeDtypeStruct((PACK, half_width), factor_u.dtype)] * paired,
        in_specs=[hbm, hbm],
        out_specs=[vmem] * (1 + paired),
        scratch_shapes=[
            pltpu.VMEM(factor_u.shape, factor_u.dtype),
            pltpu.VMEM(factor_v.shape, factor_v.dtype),
            pltpu.SemaphoreType.DMA((2, chunks)),
        ],
        compiler_params=pltpu.CompilerParams(vmem_limit_bytes=PACK_VMEM),
    )(factor_u, factor_v)
    def head_step(lengths):
        return pl.pallas_call(
            head_kernel,
            out_shape=jax.ShapeDtypeStruct((tok_cap, tok_cap), jnp.float32),
            in_specs=[hbm, vmem],
            out_specs=vmem,
            compiler_params=score_params,
            cost_estimate=pl.CostEstimate(
                flops=1, bytes_accessed=1, transcendentals=0
            ),
        )(lengths, layer_inputs)

    def norm_step(lengths, head):
        return pl.pallas_call(
            functools.partial(norm_kernel, seq_dev),
            out_shape=[
                jax.ShapeDtypeStruct((1, tok_cap), jnp.float32),
                jax.ShapeDtypeStruct((8, tok_cap), jnp.float32),
            ],
            in_specs=[hbm, vmem, vmem, vmem],
            out_specs=[vmem, vmem],
            scratch_shapes=[pltpu.SMEM(seq_lengths.shape, seq_lengths.dtype), pltpu.SemaphoreType.DMA],
            compiler_params=score_params,
            cost_estimate=pl.CostEstimate(
                flops=1, bytes_accessed=1,
                transcendentals=0,
            ),
        )(lengths, head, out_grads, layer_inputs)

    frows = devices * rank_rows
    cost = pl.CostEstimate(
        flops=1, bytes_accessed=1, transcendentals=0
    )

    def partial_step(blocks):
        arrays, places = refs_of(blocks)
        return pl.pallas_call(
            functools.partial(partial_kernel, rank_rows, paired, places),
            out_shape=jax.ShapeDtypeStruct((2, tok_cap, frows), jnp.float32),
            in_specs=[vmem] * (2 + len(arrays)),
            out_specs=vmem,
            compiler_params=score_params,
            cost_estimate=cost,
        )(out_grads, layer_inputs, *arrays)

    if paired:
        other, normed, partial = gather_blocks(
            packed[0], packed[1], devices, seq_lengths, head_step, norm_step, partial_step
        )
    else:
        normed = norm_step(seq_lengths, head_step(seq_lengths))
        gathered = lax.all_gather(packed[0], "seq", axis=0, tiled=True)
        partial = partial_step([(gathered, 2 * PACK * b) for b in range(devices)])
        other = [(gathered, 2 * PACK * b + PACK) for b in range(devices)]
    arrays, places = refs_of(other)
    return pl.pallas_call(
        functools.partial(score_kernel, rank_rows, paired, places),
        out_shape=jax.ShapeDtypeStruct((queries, seq_dev), jnp.float32),
        in_specs=[vmem] * (5 + len(arrays)),
        out_specs=vmem,
        compiler_params=score_params,
        cost_estimate=cost,
    )(*normed, partial, out_grads, layer_inputs, *arrays)


def solution(mesh):
    in_specs = (
        P(("grp", "seq"), None),
        P(("grp", "seq"), None),
        P("seq", None),
        P("seq", None),
        P("grp"),
    )
    out_specs = P(None, ("grp", "seq"))
    return jax.shard_map(local, mesh=mesh, in_specs=in_specs, out_specs=out_specs, check_vma=False)
```

```python
import functools

import jax
import jax.numpy as jnp
from jax import lax
from jax.experimental import pallas as pl
from jax.experimental.pallas import tpu as pltpu
from jax.sharding import PartitionSpec as P

RANK = 32
EPSILON = 1e-06
PACK = 16
HEAD = 8192
SCORE_VMEM = 24 * 1024 * 1024
PACK_VMEM = 58 * 1024 * 1024

NT = (((1,), (1,)), ((), ()))


def inner_rows(left, right):
    return lax.dot_general(left, right, NT, preferred_element_type=jnp.float32)


def first_half(paired):
    return lax.axis_index("grp") % 2 if paired else 0


def turn(paired, chunks):
    return lax.axis_index("seq") % chunks if paired else 0


def pack_kernel(chunks, paired, seq_dev, u_hbm, v_hbm, lengths_hbm, member_ref, both_ref, *refs):
    *own_refs, u_ref, v_ref, lengths_ref, sems = refs
    pairs = ((v_hbm, v_ref), (u_hbm, u_ref), (lengths_hbm, lengths_ref))
    copies = [pltpu.make_async_copy(hbm, ref, sems.at[i]) for i, (hbm, ref) in enumerate(pairs)]
    for copy in copies:
        copy.start()
    for copy in copies:
        copy.wait()
    seqs, tok_cap = member_ref.shape
    which = lax.broadcasted_iota(jnp.int32, (seqs, tok_cap), 0)
    position = lax.broadcasted_iota(jnp.int32, (seqs, tok_cap), 1)
    member = jnp.zeros((seqs, tok_cap), jnp.float32)
    low = 0
    for k in range(seq_dev):
        high = low + lengths_ref[lax.axis_index("seq") * seq_dev + k]
        inside = (which == k) & (position >= low) & (position < high)
        member = jnp.where(inside, 1.0, member)
        low = high
    member_ref[...] = member
    rank_rows = u_ref.shape[0]
    turned = lax.axis_index("seq") % chunks
    wide_u, wide_v = u_ref.shape[1] // (2 * chunks), v_ref.shape[1] // (2 * chunks)
    for side in range(2):
        half = first_half(paired) ^ side
        place = 0
        for ref, wide in ((u_ref, wide_u), (v_ref, wide_v)):
            rows = []
            for g in range(chunks):
                start = pl.multiple_of(((g ^ turned) * 2 + half) * wide, 128)
                rows.append(ref[:, pl.ds(start, wide)].astype(jnp.float32))
            piece = jnp.concatenate(rows, axis=0).astype(both_ref.dtype)
            both_ref[side * PACK : (side + 1) * PACK, place : place + wide] = piece
            if side == 0:
                for own_ref in own_refs:
                    own_ref[:, place : place + wide] = piece
            place += wide


def head_kernel(member_ref, in_ref, gram_ref):
    head = in_ref[:, :HEAD]
    gram_ref[...] = inner_rows(head, head)


def norm_kernel(member_ref, head_ref, out_ref, in_ref, norm_ref):
    tail = in_ref[:, HEAD:]
    paired = inner_rows(out_ref[...], out_ref[...]) * (head_ref[...] + inner_rows(tail, tail))
    member = member_ref[...]
    which = lax.broadcasted_iota(jnp.int32, member.shape, 0)
    position = lax.broadcasted_iota(jnp.int32, member.shape, 1)
    sums = jnp.dot(
        member, paired, precision=lax.Precision.HIGHEST, preferred_element_type=jnp.float32
    )
    value = jnp.sum(sums * member, axis=1, keepdims=True) / (out_ref.shape[1] * in_ref.shape[1])
    norm_ref[...] = jnp.sum(jnp.where(which == position, value, 0.0), axis=0, keepdims=True)


def swap_groups(value, bit, rank_rows):
    lanes = lax.broadcasted_iota(jnp.int32, (1, value.shape[1]), 1)
    shift = bit * rank_rows
    up = pltpu.roll(value, shift, 1)
    down = pltpu.roll(value, value.shape[1] - shift, 1)
    return jnp.where((lanes // shift) % 2 == 0, down, up)


def merged_rows(blocks, offset, wide, j, chunks, rank_rows):
    group = lax.broadcasted_iota(jnp.int32, (PACK, wide), 0) // rank_rows
    rows = []
    for first in range(0, len(blocks), chunks):
        merged = None
        for g in range(chunks):
            ref, row = blocks[first + (g ^ j)]
            piece = ref[row : row + PACK, offset : offset + wide]
            merged = piece if merged is None else jnp.where(group == g, piece, merged)
        rows.append(merged)
    return jnp.concatenate(rows, axis=0)


def both_projections(out_ref, in_ref, half, blocks, rank_rows, paired):
    chunks = PACK // rank_rows
    results, offset = [], 0
    for ref in (out_ref, in_ref):
        wide = ref.shape[1] // (2 * chunks)
        result = None
        for j in range(chunks):
            rows = merged_rows(blocks, offset, wide, j, chunks, rank_rows)
            start = pl.multiple_of(((j ^ turn(paired, chunks)) * 2 + half) * wide, 128)
            part = inner_rows(ref[:, pl.ds(start, wide)], rows)
            bit = 1
            while bit < chunks:
                if j & bit:
                    part = swap_groups(part, bit, rank_rows)
                bit *= 2
            result = part if result is None else result + part
        results.append(result)
        offset += wide
    return results


def partial_kernel(rank_rows, paired, places, out_ref, in_ref, *refs):
    *array_refs, held_ref = refs
    blocks = [(array_refs[i], row) for i, row in places]
    half = first_half(paired)
    held_out, held_in = both_projections(
        out_ref, in_ref, half, blocks, rank_rows, paired
    )
    held_ref[0] = held_out
    held_ref[1] = held_in


def score_kernel(rank_rows, paired, places, norm_ref, member_ref, held_ref, out_ref, in_ref, *refs):
    *array_refs, score_ref = refs
    blocks = [(array_refs[i], row) for i, row in places]
    half = 1 - first_half(paired)
    held_out, held_in = both_projections(
        out_ref, in_ref, half, blocks, rank_rows, paired
    )
    product = (held_ref[0] + held_out) * (held_ref[1] + held_in)
    me = lax.axis_index("seq")
    lanes = lax.broadcasted_iota(jnp.int32, (1, product.shape[1]), 1)
    source = lanes // rank_rows
    if paired:
        source = source ^ me
    query = (source * rank_rows) // RANK
    sums = jnp.dot(
        member_ref[...], product, precision=lax.Precision.HIGHEST, preferred_element_type=jnp.float32
    )
    seqs, tok_cap = member_ref.shape
    diagonal = lax.broadcasted_iota(jnp.int32, (seqs, tok_cap), 0) == lax.broadcasted_iota(
        jnp.int32, (seqs, tok_cap), 1
    )
    scale = jnp.sqrt(norm_ref[...] + EPSILON)
    for q in range(score_ref.shape[0]):
        value = jnp.sum(jnp.where(query == q, sums, 0.0), axis=1, keepdims=True)
        row = jnp.sum(jnp.where(diagonal, value, 0.0), axis=0, keepdims=True) / scale
        score_ref[q : q + 1, :] = row[:, : score_ref.shape[1]]


def gather_blocks(both, own, devices, member, head_step, norm_step, partial_step):
    def swap(value, mask):
        return lax.ppermute(value, "seq", [(i, i ^ mask) for i in range(devices)])

    def across(value):
        return lax.ppermute(value, "grp", [(0, 1), (1, 0)])

    gate = lambda *values: lax.optimization_barrier(values)
    stack = lambda *values: jnp.concatenate(values, axis=0)
    z1, z2, y0, both_core = swap(own, 4), swap(own, 8), swap(both, 2), swap(both, 1)
    z1, both_core, own = gate(z1, both_core, own)
    x1, y1, z3 = across(z1), swap(z1, 2), swap(own, 12)
    z2, x1, y1, y0, member = gate(z2, x1, y1, y0, member)
    x_near, y2 = across(stack(z2, y1)), swap(z2, 2)
    head = head_step(member)
    z3, y2, head, member = gate(z3, y2, head, member)
    x_far, y3 = across(stack(z3, y2)), swap(z3, 2)
    early = stack(y0, z1, y1, z2, x1)
    early_core = swap(early, 1)
    norms = norm_step(member, head)
    y3, norms = gate(y3, norms)
    x_last = across(y3)
    middle = stack(y2, z3, y3, x_near)
    middle_core = swap(middle, 1)
    mine, other = {}, {}

    def place(group, core, places):
        for i, (held, b) in enumerate(places):
            held[b], held[b + 1] = (group, i * PACK), (core, i * PACK)

    place(both, both_core, ((mine, 0), (other, 0)))
    place(early, early_core, ((mine, 2), (other, 2), (mine, 4), (mine, 6), (mine, 8), (other, 4)))
    place(middle, middle_core, ((mine, 10), (mine, 12), (mine, 14), (other, 8), (other, 6)))
    partial = partial_step([mine[b] for b in range(devices)])
    x_last, partial = gate(x_last, partial)
    late = stack(x_far, x_last)
    place(late, swap(late, 1), ((other, 12), (other, 10), (other, 14)))
    return [other[b] for b in range(devices)], norms, partial


def refs_of(blocks):
    arrays, places = [], []
    for value, row in blocks:
        seen = [i for i, array in enumerate(arrays) if array is value]
        if not seen:
            arrays.append(value)
        places.append((seen[0] if seen else len(arrays) - 1, row))
    return arrays, tuple(places)


def local(out_grads, layer_inputs, factor_u, factor_v, seq_lengths):
    devices = lax.axis_size("seq")
    paired = devices == 16 and lax.axis_size("grp") == 2
    seq_dev = seq_lengths.shape[0] // devices
    rank_rows = factor_u.shape[0]
    chunks = PACK // rank_rows
    queries = rank_rows * devices // RANK
    tok_cap, width_out = out_grads.shape
    width_in = layer_inputs.shape[1]
    width = width_out + width_in
    vmem = pl.BlockSpec(memory_space=pltpu.VMEM)
    hbm = pl.BlockSpec(memory_space=pltpu.HBM)

    score_params = pltpu.CompilerParams(vmem_limit_bytes=SCORE_VMEM)
    half_width = width // (2 * chunks)
    seqs = -(-seq_dev // 8) * 8
    member, *packed = pl.pallas_call(
        functools.partial(pack_kernel, chunks, paired, seq_dev),
        out_shape=[
            jax.ShapeDtypeStruct((seqs, tok_cap), jnp.float32),
            jax.ShapeDtypeStruct((2 * PACK, half_width), factor_u.dtype),
        ]
        + [jax.ShapeDtypeStruct((PACK, half_width), factor_u.dtype)] * paired,
        in_specs=[hbm] * 3,
        out_specs=[vmem] * (2 + paired),
        scratch_shapes=[
            pltpu.VMEM(factor_u.shape, factor_u.dtype),
            pltpu.VMEM(factor_v.shape, factor_v.dtype),
            pltpu.SMEM(seq_lengths.shape, seq_lengths.dtype),
            pltpu.SemaphoreType.DMA((3,)),
        ],
        compiler_params=pltpu.CompilerParams(vmem_limit_bytes=PACK_VMEM),
    )(factor_u, factor_v, seq_lengths)

    tiny = pl.CostEstimate(flops=1, bytes_accessed=1, transcendentals=0)

    def head_step(member):
        return pl.pallas_call(
            head_kernel,
            out_shape=jax.ShapeDtypeStruct((tok_cap, tok_cap), jnp.float32),
            in_specs=[vmem] * 2,
            out_specs=vmem,
            compiler_params=score_params,
            cost_estimate=tiny,
        )(member, layer_inputs)

    def norm_step(member, head):
        return pl.pallas_call(
            norm_kernel,
            out_shape=jax.ShapeDtypeStruct((1, tok_cap), jnp.float32),
            in_specs=[vmem] * 4,
            out_specs=vmem,
            compiler_params=score_params,
            cost_estimate=tiny,
        )(member, head, out_grads, layer_inputs)

    frows = devices * rank_rows
    def partial_step(blocks):
        arrays, places = refs_of(blocks)
        return pl.pallas_call(
            functools.partial(partial_kernel, rank_rows, paired, places),
            out_shape=jax.ShapeDtypeStruct((2, tok_cap, frows), jnp.float32),
            in_specs=[vmem] * (2 + len(arrays)),
            out_specs=vmem,
            compiler_params=score_params,
            cost_estimate=tiny,
        )(out_grads, layer_inputs, *arrays)

    if paired:
        other, norms, partial = gather_blocks(
            packed[0], packed[1], devices, member, head_step, norm_step, partial_step
        )
    else:
        norms = norm_step(member, head_step(member))
        gathered = lax.all_gather(packed[0], "seq", axis=0, tiled=True)
        partial = partial_step([(gathered, 2 * PACK * b) for b in range(devices)])
        other = [(gathered, 2 * PACK * b + PACK) for b in range(devices)]
    arrays, places = refs_of(other)
    return pl.pallas_call(
        functools.partial(score_kernel, rank_rows, paired, places),
        out_shape=jax.ShapeDtypeStruct((queries, seq_dev), jnp.float32),
        in_specs=[vmem] * (5 + len(arrays)),
        out_specs=vmem,
        compiler_params=score_params,
        cost_estimate=tiny,
    )(norms, member, partial, out_grads, layer_inputs, *arrays)


def solution(mesh):
    in_specs = (
        P(("grp", "seq"), None),
        P(("grp", "seq"), None),
        P("seq", None),
        P("seq", None),
        P("grp"),
    )
    out_specs = P(None, ("grp", "seq"))
    return jax.shard_map(local, mesh=mesh, in_specs=in_specs, out_specs=out_specs, check_vma=False)
```

```python
import functools

import jax
import jax.numpy as jnp
from jax import lax
from jax.experimental import pallas as pl
from jax.experimental.pallas import tpu as pltpu
from jax.sharding import PartitionSpec as P

RANK = 32
EPSILON = 1e-06
PACK = 16
HEAD = 8192
SCORE_VMEM = 24 * 1024 * 1024

NT = (((1,), (1,)), ((), ()))


def inner_rows(left, right):
    return lax.dot_general(left, right, NT, preferred_element_type=jnp.float32)


def first_half(paired):
    return lax.axis_index("grp") % 2 if paired else 0


def turn(paired, chunks):
    return lax.axis_index("seq") % chunks if paired else 0


def pack_kernel(chunks, paired, u_ref, v_ref, both_ref, *own_refs):
    rank_rows = u_ref.shape[0]
    turned = lax.axis_index("seq") % chunks
    wide_u, wide_v = u_ref.shape[1] // (2 * chunks), v_ref.shape[1] // (2 * chunks)
    for side in range(2):
        half = first_half(paired) ^ side
        place = 0
        for ref, wide in ((u_ref, wide_u), (v_ref, wide_v)):
            rows = []
            for g in range(chunks):
                start = pl.multiple_of(((g ^ turned) * 2 + half) * wide, 128)
                rows.append(ref[:, pl.ds(start, wide)].astype(jnp.float32))
            piece = jnp.concatenate(rows, axis=0).astype(both_ref.dtype)
            both_ref[side * PACK : (side + 1) * PACK, place : place + wide] = piece
            if side == 0:
                for own_ref in own_refs:
                    own_ref[:, place : place + wide] = piece
            place += wide


def head_kernel(seq_dev, lengths_hbm, in_ref, gram_ref, member_ref, lengths_ref, sem):
    copy = pltpu.make_async_copy(lengths_hbm, lengths_ref, sem)
    copy.start()
    head = in_ref[:, :HEAD]
    gram_ref[...] = inner_rows(head, head)
    copy.wait()
    seqs, tok_cap = member_ref.shape
    which = lax.broadcasted_iota(jnp.int32, (seqs, tok_cap), 0)
    position = lax.broadcasted_iota(jnp.int32, (seqs, tok_cap), 1)
    member = jnp.zeros((seqs, tok_cap), jnp.float32)
    low = 0
    for k in range(seq_dev):
        high = low + lengths_ref[lax.axis_index("seq") * seq_dev + k]
        inside = (which == k) & (position >= low) & (position < high)
        member = jnp.where(inside, 1.0, member)
        low = high
    member_ref[...] = member


def norm_kernel(member_ref, head_ref, out_ref, in_ref, norm_ref):
    tail = in_ref[:, HEAD:]
    paired = inner_rows(out_ref[...], out_ref[...]) * (head_ref[...] + inner_rows(tail, tail))
    member = member_ref[...]
    which = lax.broadcasted_iota(jnp.int32, member.shape, 0)
    position = lax.broadcasted_iota(jnp.int32, member.shape, 1)
    sums = jnp.dot(
        member, paired, precision=lax.Precision.HIGHEST, preferred_element_type=jnp.float32
    )
    value = jnp.sum(sums * member, axis=1, keepdims=True) / (out_ref.shape[1] * in_ref.shape[1])
    norm_ref[...] = jnp.sum(jnp.where(which == position, value, 0.0), axis=0, keepdims=True)


def swap_groups(value, bit, rank_rows):
    lanes = lax.broadcasted_iota(jnp.int32, (1, value.shape[1]), 1)
    shift = bit * rank_rows
    up = pltpu.roll(value, shift, 1)
    down = pltpu.roll(value, value.shape[1] - shift, 1)
    return jnp.where((lanes // shift) % 2 == 0, down, up)


def merged_rows(blocks, offset, wide, j, chunks, rank_rows):
    group = lax.broadcasted_iota(jnp.int32, (PACK, wide), 0) // rank_rows
    rows = []
    for first in range(0, len(blocks), chunks):
        merged = None
        for g in range(chunks):
            ref, row = blocks[first + (g ^ j)]
            piece = ref[row : row + PACK, offset : offset + wide]
            merged = piece if merged is None else jnp.where(group == g, piece, merged)
        rows.append(merged)
    return jnp.concatenate(rows, axis=0)


def both_projections(out_ref, in_ref, half, blocks, rank_rows, paired):
    chunks = PACK // rank_rows
    results, offset = [], 0
    for ref in (out_ref, in_ref):
        wide = ref.shape[1] // (2 * chunks)
        result = None
        for j in range(chunks):
            rows = merged_rows(blocks, offset, wide, j, chunks, rank_rows)
            start = pl.multiple_of(((j ^ turn(paired, chunks)) * 2 + half) * wide, 128)
            part = inner_rows(ref[:, pl.ds(start, wide)], rows)
            bit = 1
            while bit < chunks:
                if j & bit:
                    part = swap_groups(part, bit, rank_rows)
                bit *= 2
            result = part if result is None else result + part
        results.append(result)
        offset += wide
    return results


def partial_kernel(rank_rows, paired, places, out_ref, in_ref, *refs):
    *array_refs, held_ref = refs
    blocks = [(array_refs[i], row) for i, row in places]
    half = first_half(paired)
    held_out, held_in = both_projections(
        out_ref, in_ref, half, blocks, rank_rows, paired
    )
    held_ref[0] = held_out
    held_ref[1] = held_in


def score_kernel(rank_rows, paired, places, norm_ref, member_ref, held_ref, out_ref, in_ref, *refs):
    *array_refs, score_ref = refs
    blocks = [(array_refs[i], row) for i, row in places]
    half = 1 - first_half(paired)
    held_out, held_in = both_projections(
        out_ref, in_ref, half, blocks, rank_rows, paired
    )
    product = (held_ref[0] + held_out) * (held_ref[1] + held_in)
    me = lax.axis_index("seq")
    lanes = lax.broadcasted_iota(jnp.int32, (1, product.shape[1]), 1)
    source = lanes // rank_rows
    if paired:
        source = source ^ me
    query = (source * rank_rows) // RANK
    sums = jnp.dot(
        member_ref[...], product, precision=lax.Precision.HIGHEST, preferred_element_type=jnp.float32
    )
    seqs, tok_cap = member_ref.shape
    diagonal = lax.broadcasted_iota(jnp.int32, (seqs, tok_cap), 0) == lax.broadcasted_iota(
        jnp.int32, (seqs, tok_cap), 1
    )
    scale = jnp.sqrt(norm_ref[...] + EPSILON)
    for q in range(score_ref.shape[0]):
        value = jnp.sum(jnp.where(query == q, sums, 0.0), axis=1, keepdims=True)
        row = jnp.sum(jnp.where(diagonal, value, 0.0), axis=0, keepdims=True) / scale
        score_ref[q : q + 1, :] = row[:, : score_ref.shape[1]]


def gather_blocks(both, own, devices, lengths, head_step, norm_step, partial_step):
    def swap(value, mask):
        return lax.ppermute(value, "seq", [(i, i ^ mask) for i in range(devices)])

    def across(value):
        return lax.ppermute(value, "grp", [(0, 1), (1, 0)])

    gate = lambda *values: lax.optimization_barrier(values)
    stack = lambda *values: jnp.concatenate(values, axis=0)
    z1, z2, y0, both_core = swap(own, 4), swap(own, 8), swap(both, 2), swap(both, 1)
    z1, both_core, own = gate(z1, both_core, own)
    x1, y1, z3 = across(z1), swap(z1, 2), swap(own, 12)
    z2, y1, y0, lengths = gate(z2, y1, y0, lengths)
    x_near, y2 = across(stack(z2, y1)), swap(z2, 2)
    head, member = head_step(lengths)
    z3, y2, head, member = gate(z3, y2, head, member)
    x_far, y3 = across(stack(z3, y2)), swap(z3, 2)
    early = stack(y0, z1, y1, z2, x1)
    early_core = swap(early, 1)
    norms = norm_step(member, head)
    y3, norms = gate(y3, norms)
    x_last = across(y3)
    middle = stack(y2, z3, y3, x_near)
    middle_core = swap(middle, 1)
    mine, other = {}, {}

    def place(group, core, places):
        for i, (held, b) in enumerate(places):
            held[b], held[b + 1] = (group, i * PACK), (core, i * PACK)

    place(both, both_core, ((mine, 0), (other, 0)))
    place(early, early_core, ((mine, 2), (other, 2), (mine, 4), (mine, 6), (mine, 8), (other, 4)))
    place(middle, middle_core, ((mine, 10), (mine, 12), (mine, 14), (other, 8), (other, 6)))
    partial = partial_step([mine[b] for b in range(devices)])
    x_last, partial = gate(x_last, partial)
    late = stack(x_far, x_last)
    place(late, swap(late, 1), ((other, 12), (other, 10), (other, 14)))
    return [other[b] for b in range(devices)], norms, member, partial


def refs_of(blocks):
    arrays, places = [], []
    for value, row in blocks:
        seen = [i for i, array in enumerate(arrays) if array is value]
        if not seen:
            arrays.append(value)
        places.append((seen[0] if seen else len(arrays) - 1, row))
    return arrays, tuple(places)


def local(out_grads, layer_inputs, factor_u, factor_v, seq_lengths):
    devices = lax.axis_size("seq")
    paired = devices == 16 and lax.axis_size("grp") == 2
    seq_dev = seq_lengths.shape[0] // devices
    rank_rows = factor_u.shape[0]
    chunks = PACK // rank_rows
    queries = rank_rows * devices // RANK
    tok_cap, width_out = out_grads.shape
    width_in = layer_inputs.shape[1]
    width = width_out + width_in
    vmem = pl.BlockSpec(memory_space=pltpu.VMEM)
    hbm = pl.BlockSpec(memory_space=pltpu.HBM)

    score_params = pltpu.CompilerParams(vmem_limit_bytes=SCORE_VMEM)
    half_width = width // (2 * chunks)
    seqs = -(-seq_dev // 8) * 8
    packed = pl.pallas_call(
        functools.partial(pack_kernel, chunks, paired),
        out_shape=[jax.ShapeDtypeStruct((2 * PACK, half_width), factor_u.dtype)]
        + [jax.ShapeDtypeStruct((PACK, half_width), factor_u.dtype)] * paired,
        in_specs=[vmem] * 2,
        out_specs=[vmem] * (1 + paired),
        compiler_params=score_params,
    )(factor_u, factor_v)

    tiny = pl.CostEstimate(flops=1, bytes_accessed=1, transcendentals=0)

    def head_step(lengths):
        return pl.pallas_call(
            functools.partial(head_kernel, seq_dev),
            out_shape=[
                jax.ShapeDtypeStruct((tok_cap, tok_cap), jnp.float32),
                jax.ShapeDtypeStruct((seqs, tok_cap), jnp.float32),
            ],
            in_specs=[hbm, vmem],
            out_specs=[vmem] * 2,
            scratch_shapes=[pltpu.SMEM(lengths.shape, lengths.dtype), pltpu.SemaphoreType.DMA],
            compiler_params=score_params,
            cost_estimate=tiny,
        )(lengths, layer_inputs)

    def norm_step(member, head):
        return pl.pallas_call(
            norm_kernel,
            out_shape=jax.ShapeDtypeStruct((1, tok_cap), jnp.float32),
            in_specs=[vmem] * 4,
            out_specs=vmem,
            compiler_params=score_params,
            cost_estimate=tiny,
        )(member, head, out_grads, layer_inputs)

    frows = devices * rank_rows
    def partial_step(blocks):
        arrays, places = refs_of(blocks)
        return pl.pallas_call(
            functools.partial(partial_kernel, rank_rows, paired, places),
            out_shape=jax.ShapeDtypeStruct((2, tok_cap, frows), jnp.float32),
            in_specs=[vmem] * (2 + len(arrays)),
            out_specs=vmem,
            compiler_params=score_params,
            cost_estimate=tiny,
        )(out_grads, layer_inputs, *arrays)

    if paired:
        other, norms, member, partial = gather_blocks(
            packed[0], packed[1], devices, seq_lengths, head_step, norm_step, partial_step
        )
    else:
        head, member = head_step(seq_lengths)
        norms = norm_step(member, head)
        gathered = lax.all_gather(packed[0], "seq", axis=0, tiled=True)
        partial = partial_step([(gathered, 2 * PACK * b) for b in range(devices)])
        other = [(gathered, 2 * PACK * b + PACK) for b in range(devices)]
    arrays, places = refs_of(other)
    return pl.pallas_call(
        functools.partial(score_kernel, rank_rows, paired, places),
        out_shape=jax.ShapeDtypeStruct((queries, seq_dev), jnp.float32),
        in_specs=[vmem] * (5 + len(arrays)),
        out_specs=vmem,
        compiler_params=score_params,
        cost_estimate=tiny,
    )(norms, member, partial, out_grads, layer_inputs, *arrays)


def solution(mesh):
    in_specs = (
        P(("grp", "seq"), None),
        P(("grp", "seq"), None),
        P("seq", None),
        P("seq", None),
        P("grp"),
    )
    out_specs = P(None, ("grp", "seq"))
    return jax.shard_map(local, mesh=mesh, in_specs=in_specs, out_specs=out_specs, check_vma=False)
```

```python
import functools

import jax
import jax.numpy as jnp
from jax import lax
from jax.experimental import pallas as pl
from jax.experimental.pallas import tpu as pltpu
from jax.sharding import PartitionSpec as P

RANK = 32
EPSILON = 1e-06
PACK = 16
HEAD = 8192
SCORE_VMEM = 24 * 1024 * 1024

NT = (((1,), (1,)), ((), ()))


def inner_rows(left, right):
    return lax.dot_general(left, right, NT, preferred_element_type=jnp.float32)


def first_half(paired):
    return lax.axis_index("grp") % 2 if paired else 0


def turn(paired, chunks):
    return lax.axis_index("seq") % chunks if paired else 0


def pack_kernel(chunks, paired, u_ref, v_ref, both_ref, *own_refs):
    rank_rows = u_ref.shape[0]
    turned = lax.axis_index("seq") % chunks
    wide_u, wide_v = u_ref.shape[1] // (2 * chunks), v_ref.shape[1] // (2 * chunks)
    for side in range(2):
        half = first_half(paired) ^ side
        place = 0
        for ref, wide in ((u_ref, wide_u), (v_ref, wide_v)):
            rows = []
            for g in range(chunks):
                start = pl.multiple_of(((g ^ turned) * 2 + half) * wide, 128)
                rows.append(ref[:, pl.ds(start, wide)].astype(jnp.float32))
            piece = jnp.concatenate(rows, axis=0).astype(both_ref.dtype)
            both_ref[side * PACK : (side + 1) * PACK, place : place + wide] = piece
            if side == 0:
                for own_ref in own_refs:
                    own_ref[:, place : place + wide] = piece
            place += wide


def head_kernel(seq_dev, lengths_hbm, in_ref, gram_ref, member_ref, spread_ref, lengths_ref, sem):
    copy = pltpu.make_async_copy(lengths_hbm, lengths_ref, sem)
    copy.start()
    head = in_ref[:, :HEAD]
    gram_ref[...] = inner_rows(head, head)
    copy.wait()
    seqs, tok_cap = member_ref.shape
    which = lax.broadcasted_iota(jnp.int32, (seqs, tok_cap), 0)
    position = lax.broadcasted_iota(jnp.int32, (seqs, tok_cap), 1)
    member = jnp.zeros((seqs, tok_cap), jnp.float32)
    rows = lax.broadcasted_iota(jnp.int32, spread_ref.shape[1:], 0)
    low = 0
    for k in range(seq_dev):
        high = low + lengths_ref[lax.axis_index("seq") * seq_dev + k]
        inside = (which == k) & (position >= low) & (position < high)
        member = jnp.where(inside, 1.0, member)
        spread_ref[k] = ((rows >= low) & (rows < high)).astype(jnp.float32)
        low = high
    member_ref[...] = member


def norm_kernel(member_ref, head_ref, out_ref, in_ref, norm_ref):
    tail = in_ref[:, HEAD:]
    paired = inner_rows(out_ref[...], out_ref[...]) * (head_ref[...] + inner_rows(tail, tail))
    member = member_ref[...]
    which = lax.broadcasted_iota(jnp.int32, member.shape, 0)
    position = lax.broadcasted_iota(jnp.int32, member.shape, 1)
    sums = jnp.dot(
        member, paired, precision=lax.Precision.HIGHEST, preferred_element_type=jnp.float32
    )
    value = jnp.sum(sums * member, axis=1, keepdims=True) / (out_ref.shape[1] * in_ref.shape[1])
    norm_ref[...] = jnp.sum(jnp.where(which == position, value, 0.0), axis=0, keepdims=True)


def swap_groups(value, bit, rank_rows):
    lanes = lax.broadcasted_iota(jnp.int32, (1, value.shape[1]), 1)
    shift = bit * rank_rows
    up = pltpu.roll(value, shift, 1)
    down = pltpu.roll(value, value.shape[1] - shift, 1)
    return jnp.where((lanes // shift) % 2 == 0, down, up)


def merged_rows(blocks, offset, wide, j, chunks, rank_rows):
    group = lax.broadcasted_iota(jnp.int32, (PACK, wide), 0) // rank_rows
    rows = []
    for first in range(0, len(blocks), chunks):
        merged = None
        for g in range(chunks):
            ref, row = blocks[first + (g ^ j)]
            piece = ref[row : row + PACK, offset : offset + wide]
            merged = piece if merged is None else jnp.where(group == g, piece, merged)
        rows.append(merged)
    return jnp.concatenate(rows, axis=0)


def both_projections(out_ref, in_ref, half, blocks, rank_rows, paired):
    chunks = PACK // rank_rows
    results, offset = [], 0
    for ref in (out_ref, in_ref):
        wide = ref.shape[1] // (2 * chunks)
        result = None
        for j in reversed(range(chunks)):
            rows = merged_rows(blocks, offset, wide, j, chunks, rank_rows)
            start = pl.multiple_of(((j ^ turn(paired, chunks)) * 2 + half) * wide, 128)
            part = inner_rows(ref[:, pl.ds(start, wide)], rows)
            bit = 1
            while bit < chunks:
                if j & bit:
                    part = swap_groups(part, bit, rank_rows)
                bit *= 2
            result = part if result is None else result + part
        results.append(result)
        offset += wide
    return results


def partial_kernel(rank_rows, paired, places, out_ref, in_ref, *refs):
    *array_refs, held_ref = refs
    blocks = [(array_refs[i], row) for i, row in places]
    half = first_half(paired)
    held_out, held_in = both_projections(
        out_ref, in_ref, half, blocks, rank_rows, paired
    )
    held_ref[0] = held_out
    held_ref[1] = held_in


def score_kernel(rank_rows, paired, places, norm_ref, spread_ref, held_ref, out_ref, in_ref, *refs):
    *array_refs, score_ref = refs
    blocks = [(array_refs[i], row) for i, row in places]
    half = 1 - first_half(paired)
    held_out, held_in = both_projections(
        out_ref, in_ref, half, blocks, rank_rows, paired
    )
    product = (held_ref[0] + held_out) * (held_ref[1] + held_in)
    me = lax.axis_index("seq")
    lanes = lax.broadcasted_iota(jnp.int32, (1, product.shape[1]), 1)
    source = lanes // rank_rows
    if paired:
        source = source ^ me
    query = (source * rank_rows) // RANK
    seqs, tok_cap = -(-spread_ref.shape[0] // 8) * 8, spread_ref.shape[1]
    which = lax.broadcasted_iota(jnp.int32, (seqs, product.shape[1]), 0)
    sums = jnp.zeros(which.shape, jnp.float32)
    for k in range(spread_ref.shape[0]):
        sums = jnp.where(which == k, jnp.sum(product * spread_ref[k], axis=0, keepdims=True), sums)
    diagonal = lax.broadcasted_iota(jnp.int32, (seqs, tok_cap), 0) == lax.broadcasted_iota(
        jnp.int32, (seqs, tok_cap), 1
    )
    scale = jnp.sqrt(norm_ref[...] + EPSILON)
    for q in range(score_ref.shape[0]):
        value = jnp.sum(jnp.where(query == q, sums, 0.0), axis=1, keepdims=True)
        row = jnp.sum(jnp.where(diagonal, value, 0.0), axis=0, keepdims=True) / scale
        score_ref[q : q + 1, :] = row[:, : score_ref.shape[1]]


def gather_blocks(both, own, devices, lengths, head_step, norm_step, partial_step):
    def swap(value, mask):
        return lax.ppermute(value, "seq", [(i, i ^ mask) for i in range(devices)])

    def across(value):
        return lax.ppermute(value, "grp", [(0, 1), (1, 0)])

    gate = lambda *values: lax.optimization_barrier(values)
    stack = lambda *values: jnp.concatenate(values, axis=0)
    z1, z2, y0, both_core = swap(own, 4), swap(own, 8), swap(both, 2), swap(both, 1)
    z1, both_core, own = gate(z1, both_core, own)
    x1, y1, z3 = across(z1), swap(z1, 2), swap(own, 12)
    z2, y1, y0, lengths = gate(z2, y1, y0, lengths)
    x_near, y2 = across(stack(z2, y1)), swap(z2, 2)
    head, member, spread = head_step(lengths)
    z3, y2, head, member = gate(z3, y2, head, member)
    x_far, y3 = across(stack(z3, y2)), swap(z3, 2)
    early = stack(y0, z1, y1, z2, x1)
    early_core = swap(early, 1)
    y3, member = gate(y3, member)
    x_last = across(y3)
    norms = norm_step(member, head)
    middle = stack(y2, z3, y3, x_near)
    middle_core = swap(middle, 1)
    mine, other = {}, {}

    def place(group, core, places):
        for i, (held, b) in enumerate(places):
            held[b], held[b + 1] = (group, i * PACK), (core, i * PACK)

    place(both, both_core, ((mine, 0), (other, 0)))
    place(early, early_core, ((mine, 2), (other, 2), (mine, 4), (mine, 6), (mine, 8), (other, 4)))
    place(middle, middle_core, ((mine, 10), (mine, 12), (mine, 14), (other, 8), (other, 6)))
    partial = partial_step([mine[b] for b in range(devices)])
    x_last, partial, norms = gate(x_last, partial, norms)
    late = stack(x_far, x_last)
    place(late, swap(late, 1), ((other, 12), (other, 10), (other, 14)))
    return [other[b] for b in range(devices)], norms, spread, partial


def refs_of(blocks):
    arrays, places = [], []
    for value, row in blocks:
        seen = [i for i, array in enumerate(arrays) if array is value]
        if not seen:
            arrays.append(value)
        places.append((seen[0] if seen else len(arrays) - 1, row))
    return arrays, tuple(places)


def local(out_grads, layer_inputs, factor_u, factor_v, seq_lengths):
    devices = lax.axis_size("seq")
    paired = devices == 16 and lax.axis_size("grp") == 2
    seq_dev = seq_lengths.shape[0] // devices
    rank_rows = factor_u.shape[0]
    chunks = PACK // rank_rows
    queries = rank_rows * devices // RANK
    tok_cap, width_out = out_grads.shape
    width_in = layer_inputs.shape[1]
    width = width_out + width_in
    vmem = pl.BlockSpec(memory_space=pltpu.VMEM)
    hbm = pl.BlockSpec(memory_space=pltpu.HBM)

    score_params = pltpu.CompilerParams(vmem_limit_bytes=SCORE_VMEM)
    half_width = width // (2 * chunks)
    seqs = -(-seq_dev // 8) * 8
    packed = pl.pallas_call(
        functools.partial(pack_kernel, chunks, paired),
        out_shape=[jax.ShapeDtypeStruct((2 * PACK, half_width), factor_u.dtype)]
        + [jax.ShapeDtypeStruct((PACK, half_width), factor_u.dtype)] * paired,
        in_specs=[vmem] * 2,
        out_specs=[vmem] * (1 + paired),
        compiler_params=score_params,
    )(factor_u, factor_v)

    frows = devices * rank_rows
    tiny = pl.CostEstimate(flops=1, bytes_accessed=1, transcendentals=0)

    def head_step(lengths):
        return pl.pallas_call(
            functools.partial(head_kernel, seq_dev),
            out_shape=[
                jax.ShapeDtypeStruct((tok_cap, tok_cap), jnp.float32),
                jax.ShapeDtypeStruct((seqs, tok_cap), jnp.float32),
                jax.ShapeDtypeStruct((seq_dev, tok_cap, frows), jnp.float32),
            ],
            in_specs=[hbm, vmem],
            out_specs=[vmem] * 3,
            scratch_shapes=[pltpu.SMEM(lengths.shape, lengths.dtype), pltpu.SemaphoreType.DMA],
            compiler_params=score_params,
            cost_estimate=tiny,
        )(lengths, layer_inputs)

    def norm_step(member, head):
        return pl.pallas_call(
            norm_kernel,
            out_shape=jax.ShapeDtypeStruct((1, tok_cap), jnp.float32),
            in_specs=[vmem] * 4,
            out_specs=vmem,
            compiler_params=score_params,
            cost_estimate=tiny,
        )(member, head, out_grads, layer_inputs)

    def partial_step(blocks):
        arrays, places = refs_of(blocks)
        return pl.pallas_call(
            functools.partial(partial_kernel, rank_rows, paired, places),
            out_shape=jax.ShapeDtypeStruct((2, tok_cap, frows), jnp.float32),
            in_specs=[vmem] * (2 + len(arrays)),
            out_specs=vmem,
            compiler_params=score_params,
            cost_estimate=tiny,
        )(out_grads, layer_inputs, *arrays)

    if paired:
        other, norms, spread, partial = gather_blocks(
            packed[0], packed[1], devices, seq_lengths, head_step, norm_step, partial_step
        )
    else:
        head, member, spread = head_step(seq_lengths)
        norms = norm_step(member, head)
        gathered = lax.all_gather(packed[0], "seq", axis=0, tiled=True)
        partial = partial_step([(gathered, 2 * PACK * b) for b in range(devices)])
        other = [(gathered, 2 * PACK * b + PACK) for b in range(devices)]
    arrays, places = refs_of(other)
    return pl.pallas_call(
        functools.partial(score_kernel, rank_rows, paired, places),
        out_shape=jax.ShapeDtypeStruct((queries, seq_dev), jnp.float32),
        in_specs=[vmem] * (5 + len(arrays)),
        out_specs=vmem,
        compiler_params=score_params,
        cost_estimate=tiny,
    )(norms, spread, partial, out_grads, layer_inputs, *arrays)


def solution(mesh):
    in_specs = (
        P(("grp", "seq"), None),
        P(("grp", "seq"), None),
        P("seq", None),
        P("seq", None),
        P("grp"),
    )
    out_specs = P(None, ("grp", "seq"))
    return jax.shard_map(local, mesh=mesh, in_specs=in_specs, out_specs=out_specs, check_vma=False)
```

```python
import functools

import jax
import jax.numpy as jnp
from jax import lax
from jax.experimental import pallas as pl
from jax.experimental.pallas import tpu as pltpu
from jax.sharding import PartitionSpec as P

RANK = 32
EPSILON = 1e-06
PACK = 16
HEAD = 8192
SCORE_VMEM = 24 * 1024 * 1024

NT = (((1,), (1,)), ((), ()))


def inner_rows(left, right):
    return lax.dot_general(left, right, NT, preferred_element_type=jnp.float32)


def first_half(paired):
    return lax.axis_index("grp") % 2 if paired else 0


def turn(paired, chunks):
    return lax.axis_index("seq") % chunks if paired else 0


def pack_kernel(chunks, paired, u_ref, v_ref, both_ref, *own_refs):
    rank_rows = u_ref.shape[0]
    turned = lax.axis_index("seq") % chunks
    wide_u, wide_v = u_ref.shape[1] // (2 * chunks), v_ref.shape[1] // (2 * chunks)
    for side in range(2):
        half = first_half(paired) ^ side
        place = 0
        for ref, wide in ((u_ref, wide_u), (v_ref, wide_v)):
            rows = []
            for g in range(chunks):
                start = pl.multiple_of(((g ^ turned) * 2 + half) * wide, 128)
                rows.append(ref[:, pl.ds(start, wide)].astype(jnp.float32))
            piece = jnp.concatenate(rows, axis=0).astype(both_ref.dtype)
            both_ref[side * PACK : (side + 1) * PACK, place : place + wide] = piece
            if side == 0:
                for own_ref in own_refs:
                    own_ref[:, place : place + wide] = piece
            place += wide


def head_kernel(seq_dev, lengths_hbm, in_ref, gram_ref, member_ref, spread_ref, lengths_ref, sem):
    copy = pltpu.make_async_copy(lengths_hbm, lengths_ref, sem)
    copy.start()
    head = in_ref[:, :HEAD]
    gram_ref[...] = inner_rows(head, head)
    copy.wait()
    seqs, tok_cap = member_ref.shape
    which = lax.broadcasted_iota(jnp.int32, (seqs, tok_cap), 0)
    position = lax.broadcasted_iota(jnp.int32, (seqs, tok_cap), 1)
    member = jnp.zeros((seqs, tok_cap), jnp.float32)
    rows = lax.broadcasted_iota(jnp.int32, spread_ref.shape[1:], 0)
    low = 0
    for k in range(seq_dev):
        high = low + lengths_ref[lax.axis_index("seq") * seq_dev + k]
        inside = (which == k) & (position >= low) & (position < high)
        member = jnp.where(inside, 1.0, member)
        spread_ref[k] = ((rows >= low) & (rows < high)).astype(jnp.float32)
        low = high
    member_ref[...] = member


def norm_kernel(member_ref, head_ref, out_ref, in_ref, norm_ref):
    tail = in_ref[:, HEAD:]
    paired = inner_rows(out_ref[...], out_ref[...]) * (head_ref[...] + inner_rows(tail, tail))
    member = member_ref[...]
    which = lax.broadcasted_iota(jnp.int32, member.shape, 0)
    position = lax.broadcasted_iota(jnp.int32, member.shape, 1)
    sums = jnp.dot(
        member, paired, precision=lax.Precision.HIGHEST, preferred_element_type=jnp.float32
    )
    value = jnp.sum(sums * member, axis=1, keepdims=True) / (out_ref.shape[1] * in_ref.shape[1])
    norm_ref[...] = jnp.sum(jnp.where(which == position, value, 0.0), axis=0, keepdims=True)


def swap_groups(value, bit, rank_rows):
    lanes = lax.broadcasted_iota(jnp.int32, (1, value.shape[1]), 1)
    shift = bit * rank_rows
    up = pltpu.roll(value, shift, 1)
    down = pltpu.roll(value, value.shape[1] - shift, 1)
    return jnp.where((lanes // shift) % 2 == 0, down, up)


def merged_rows(blocks, offset, wide, j, chunks, rank_rows):
    group = lax.broadcasted_iota(jnp.int32, (PACK, wide), 0) // rank_rows
    rows = []
    for first in range(0, len(blocks), chunks):
        merged = None
        for g in range(chunks):
            ref, row = blocks[first + (g ^ j)]
            piece = ref[row : row + PACK, offset : offset + wide]
            merged = piece if merged is None else jnp.where(group == g, piece, merged)
        rows.append(merged)
    return jnp.concatenate(rows, axis=0)


def both_projections(out_ref, in_ref, half, blocks, rank_rows, paired):
    chunks = PACK // rank_rows
    results, offset = [], 0
    for ref in (out_ref, in_ref):
        wide = ref.shape[1] // (2 * chunks)
        result = None
        for j in reversed(range(chunks)):
            rows = merged_rows(blocks, offset, wide, j, chunks, rank_rows)
            start = pl.multiple_of(((j ^ turn(paired, chunks)) * 2 + half) * wide, 128)
            part = inner_rows(ref[:, pl.ds(start, wide)], rows)
            bit = 1
            while bit < chunks:
                if j & bit:
                    part = swap_groups(part, bit, rank_rows)
                bit *= 2
            result = part if result is None else result + part
        results.append(result)
        offset += wide
    return results


def partial_kernel(rank_rows, paired, places, out_ref, in_ref, *refs):
    *array_refs, held_ref = refs
    blocks = [(array_refs[i], row) for i, row in places]
    half = first_half(paired)
    held_out, held_in = both_projections(
        out_ref, in_ref, half, blocks, rank_rows, paired
    )
    held_ref[0] = held_out
    held_ref[1] = held_in


def score_kernel(rank_rows, paired, places, norm_ref, spread_ref, held_ref, out_ref, in_ref, *refs):
    *array_refs, score_ref = refs
    blocks = [(array_refs[i], row) for i, row in places]
    half = 1 - first_half(paired)
    held_out, held_in = both_projections(
        out_ref, in_ref, half, blocks, rank_rows, paired
    )
    product = (held_ref[0] + held_out) * (held_ref[1] + held_in)
    me = lax.axis_index("seq")
    lanes = lax.broadcasted_iota(jnp.int32, (1, product.shape[1]), 1)
    source = lanes // rank_rows
    if paired:
        source = source ^ me
    query = (source * rank_rows) // RANK
    seqs, tok_cap = -(-spread_ref.shape[0] // 8) * 8, spread_ref.shape[1]
    which = lax.broadcasted_iota(jnp.int32, (seqs, product.shape[1]), 0)
    sums = jnp.zeros(which.shape, jnp.float32)
    for k in range(spread_ref.shape[0]):
        sums = jnp.where(which == k, jnp.sum(product * spread_ref[k], axis=0, keepdims=True), sums)
    diagonal = lax.broadcasted_iota(jnp.int32, (seqs, tok_cap), 0) == lax.broadcasted_iota(
        jnp.int32, (seqs, tok_cap), 1
    )
    scale = jnp.sqrt(norm_ref[...] + EPSILON)
    for q in range(score_ref.shape[0]):
        value = jnp.sum(jnp.where(query == q, sums, 0.0), axis=1, keepdims=True)
        row = jnp.sum(jnp.where(diagonal, value, 0.0), axis=0, keepdims=True) / scale
        score_ref[q : q + 1, :] = row[:, : score_ref.shape[1]]


def gather_blocks(both, own, devices, lengths, head_step, norm_step, partial_step):
    def swap(value, mask):
        return lax.ppermute(value, "seq", [(i, i ^ mask) for i in range(devices)])

    def across(value):
        return lax.ppermute(value, "grp", [(0, 1), (1, 0)])

    gate = lambda *values: lax.optimization_barrier(values)
    stack = lambda *values: jnp.concatenate(values, axis=0)
    z1, z2, y0, both_core = swap(own, 4), swap(own, 8), swap(both, 2), swap(both, 1)
    z1, both_core, own = gate(z1, both_core, own)
    x1, y1, z3 = across(z1), swap(z1, 2), swap(own, 12)
    z2, y1, y0, lengths = gate(z2, y1, y0, lengths)
    x_near, y2 = across(stack(z2, y1)), swap(z2, 2)
    z3, y2, lengths = gate(z3, y2, lengths)
    head, member, spread = head_step(lengths)
    x3, y3 = across(z3), swap(z3, 2)
    early = stack(y0, z1, y1, z2, x1)
    early_core = swap(early, 1)
    x_near, head = gate(x_near, head)
    yx2 = swap(x_near[:PACK], 2)
    y3, member, head = gate(y3, member, head)
    x_last = across(y3)
    norms = norm_step(member, head)
    middle = stack(y2, z3, y3, x_near)
    middle_core = swap(middle, 1)
    mine, other = {}, {}

    def place(group, core, places):
        for i, (held, b) in enumerate(places):
            held[b], held[b + 1] = (group, i * PACK), (core, i * PACK)

    place(both, both_core, ((mine, 0), (other, 0)))
    place(early, early_core, ((mine, 2), (other, 2), (mine, 4), (mine, 6), (mine, 8), (other, 4)))
    place(middle, middle_core, ((mine, 10), (mine, 12), (mine, 14), (other, 8), (other, 6)))
    partial = partial_step([mine[b] for b in range(devices)])
    x_last, partial, norms = gate(x_last, partial, norms)
    late = stack(x3, yx2, x_last)
    place(late, swap(late, 1), ((other, 12), (other, 10), (other, 14)))
    return [other[b] for b in range(devices)], norms, spread, partial


def refs_of(blocks):
    arrays, places = [], []
    for value, row in blocks:
        seen = [i for i, array in enumerate(arrays) if array is value]
        if not seen:
            arrays.append(value)
        places.append((seen[0] if seen else len(arrays) - 1, row))
    return arrays, tuple(places)


def local(out_grads, layer_inputs, factor_u, factor_v, seq_lengths):
    devices = lax.axis_size("seq")
    paired = devices == 16 and lax.axis_size("grp") == 2
    seq_dev = seq_lengths.shape[0] // devices
    rank_rows = factor_u.shape[0]
    chunks = PACK // rank_rows
    queries = rank_rows * devices // RANK
    tok_cap, width_out = out_grads.shape
    width_in = layer_inputs.shape[1]
    width = width_out + width_in
    vmem = pl.BlockSpec(memory_space=pltpu.VMEM)
    hbm = pl.BlockSpec(memory_space=pltpu.HBM)

    score_params = pltpu.CompilerParams(vmem_limit_bytes=SCORE_VMEM)
    half_width = width // (2 * chunks)
    seqs = -(-seq_dev // 8) * 8
    packed = pl.pallas_call(
        functools.partial(pack_kernel, chunks, paired),
        out_shape=[jax.ShapeDtypeStruct((2 * PACK, half_width), factor_u.dtype)]
        + [jax.ShapeDtypeStruct((PACK, half_width), factor_u.dtype)] * paired,
        in_specs=[vmem] * 2,
        out_specs=[vmem] * (1 + paired),
        compiler_params=score_params,
    )(factor_u, factor_v)

    frows = devices * rank_rows
    tiny = pl.CostEstimate(flops=1, bytes_accessed=1, transcendentals=0)

    def head_step(lengths):
        return pl.pallas_call(
            functools.partial(head_kernel, seq_dev),
            out_shape=[
                jax.ShapeDtypeStruct((tok_cap, tok_cap), jnp.float32),
                jax.ShapeDtypeStruct((seqs, tok_cap), jnp.float32),
                jax.ShapeDtypeStruct((seq_dev, tok_cap, frows), jnp.float32),
            ],
            in_specs=[hbm, vmem],
            out_specs=[vmem] * 3,
            scratch_shapes=[pltpu.SMEM(lengths.shape, lengths.dtype), pltpu.SemaphoreType.DMA],
            compiler_params=score_params,
            cost_estimate=tiny,
        )(lengths, layer_inputs)

    def norm_step(member, head):
        return pl.pallas_call(
            norm_kernel,
            out_shape=jax.ShapeDtypeStruct((1, tok_cap), jnp.float32),
            in_specs=[vmem] * 4,
            out_specs=vmem,
            compiler_params=score_params,
            cost_estimate=tiny,
        )(member, head, out_grads, layer_inputs)

    def partial_step(blocks):
        arrays, places = refs_of(blocks)
        return pl.pallas_call(
            functools.partial(partial_kernel, rank_rows, paired, places),
            out_shape=jax.ShapeDtypeStruct((2, tok_cap, frows), jnp.float32),
            in_specs=[vmem] * (2 + len(arrays)),
            out_specs=vmem,
            compiler_params=score_params,
            cost_estimate=tiny,
        )(out_grads, layer_inputs, *arrays)

    if paired:
        other, norms, spread, partial = gather_blocks(
            packed[0], packed[1], devices, seq_lengths, head_step, norm_step, partial_step
        )
    else:
        head, member, spread = head_step(seq_lengths)
        norms = norm_step(member, head)
        gathered = lax.all_gather(packed[0], "seq", axis=0, tiled=True)
        partial = partial_step([(gathered, 2 * PACK * b) for b in range(devices)])
        other = [(gathered, 2 * PACK * b + PACK) for b in range(devices)]
    arrays, places = refs_of(other)
    return pl.pallas_call(
        functools.partial(score_kernel, rank_rows, paired, places),
        out_shape=jax.ShapeDtypeStruct((queries, seq_dev), jnp.float32),
        in_specs=[vmem] * (5 + len(arrays)),
        out_specs=vmem,
        compiler_params=score_params,
        cost_estimate=tiny,
    )(norms, spread, partial, out_grads, layer_inputs, *arrays)


def solution(mesh):
    in_specs = (
        P(("grp", "seq"), None),
        P(("grp", "seq"), None),
        P("seq", None),
        P("seq", None),
        P("grp"),
    )
    out_specs = P(None, ("grp", "seq"))
    return jax.shard_map(local, mesh=mesh, in_specs=in_specs, out_specs=out_specs, check_vma=False)
```

```python
import functools

import jax
import jax.numpy as jnp
from jax import lax
from jax.experimental import pallas as pl
from jax.experimental.pallas import tpu as pltpu
from jax.sharding import PartitionSpec as P

RANK = 32
EPSILON = 1e-06
PACK = 16
HEAD = 8192
SCORE_VMEM = 24 * 1024 * 1024

NT = (((1,), (1,)), ((), ()))


def inner_rows(left, right):
    return lax.dot_general(left, right, NT, preferred_element_type=jnp.float32)


def first_half(paired):
    return lax.axis_index("grp") % 2 if paired else 0


def turn(paired, chunks):
    return lax.axis_index("seq") % chunks if paired else 0


def pack_kernel(chunks, paired, u_ref, v_ref, both_ref, *own_refs):
    rank_rows = u_ref.shape[0]
    turned = lax.axis_index("seq") % chunks
    wide_u, wide_v = u_ref.shape[1] // (2 * chunks), v_ref.shape[1] // (2 * chunks)
    for side in range(2):
        half = first_half(paired) ^ side
        place = 0
        for ref, wide in ((u_ref, wide_u), (v_ref, wide_v)):
            rows = []
            for g in range(chunks):
                start = pl.multiple_of(((g ^ turned) * 2 + half) * wide, 128)
                rows.append(ref[:, pl.ds(start, wide)].astype(jnp.float32))
            piece = jnp.concatenate(rows, axis=0).astype(both_ref.dtype)
            both_ref[side * PACK : (side + 1) * PACK, place : place + wide] = piece
            if side == 0:
                for own_ref in own_refs:
                    own_ref[:, place : place + wide] = piece
            place += wide


def member_kernel(seq_dev, lengths_hbm, after_ref, member_ref, spread_ref, lengths_ref, sem):
    copy = pltpu.make_async_copy(lengths_hbm, lengths_ref, sem)
    copy.start()
    copy.wait()
    seqs, tok_cap = member_ref.shape
    which = lax.broadcasted_iota(jnp.int32, (seqs, tok_cap), 0)
    position = lax.broadcasted_iota(jnp.int32, (seqs, tok_cap), 1)
    member = jnp.zeros((seqs, tok_cap), jnp.float32)
    rows = lax.broadcasted_iota(jnp.int32, spread_ref.shape[1:], 0)
    low = 0
    for k in range(seq_dev):
        high = low + lengths_ref[lax.axis_index("seq") * seq_dev + k]
        inside = (which == k) & (position >= low) & (position < high)
        member = jnp.where(inside, 1.0, member)
        spread_ref[k] = ((rows >= low) & (rows < high)).astype(jnp.float32)
        low = high
    member_ref[...] = member


def head_kernel(member_ref, in_ref, gram_ref):
    head = in_ref[:, :HEAD]
    gram_ref[...] = inner_rows(head, head)


def norm_kernel(member_ref, head_ref, out_ref, in_ref, norm_ref):
    tail = in_ref[:, HEAD:]
    paired = inner_rows(out_ref[...], out_ref[...]) * (head_ref[...] + inner_rows(tail, tail))
    member = member_ref[...]
    which = lax.broadcasted_iota(jnp.int32, member.shape, 0)
    position = lax.broadcasted_iota(jnp.int32, member.shape, 1)
    sums = jnp.dot(
        member, paired, precision=lax.Precision.HIGHEST, preferred_element_type=jnp.float32
    )
    value = jnp.sum(sums * member, axis=1, keepdims=True) / (out_ref.shape[1] * in_ref.shape[1])
    norm_ref[...] = jnp.sum(jnp.where(which == position, value, 0.0), axis=0, keepdims=True)


def swap_groups(value, bit, rank_rows):
    lanes = lax.broadcasted_iota(jnp.int32, (1, value.shape[1]), 1)
    shift = bit * rank_rows
    up = pltpu.roll(value, shift, 1)
    down = pltpu.roll(value, value.shape[1] - shift, 1)
    return jnp.where((lanes // shift) % 2 == 0, down, up)


def merged_rows(blocks, offset, wide, j, chunks, rank_rows):
    group = lax.broadcasted_iota(jnp.int32, (PACK, wide), 0) // rank_rows
    rows = []
    for first in range(0, len(blocks), chunks):
        merged = None
        for g in range(chunks):
            ref, row = blocks[first + (g ^ j)]
            piece = ref[row : row + PACK, offset : offset + wide]
            merged = piece if merged is None else jnp.where(group == g, piece, merged)
        rows.append(merged)
    return jnp.concatenate(rows, axis=0)


def both_projections(out_ref, in_ref, half, blocks, rank_rows, paired):
    chunks = PACK // rank_rows
    results, offset = [], 0
    for ref in (out_ref, in_ref):
        wide = ref.shape[1] // (2 * chunks)
        result = None
        for j in reversed(range(chunks)):
            rows = merged_rows(blocks, offset, wide, j, chunks, rank_rows)
            start = pl.multiple_of(((j ^ turn(paired, chunks)) * 2 + half) * wide, 128)
            part = inner_rows(ref[:, pl.ds(start, wide)], rows)
            bit = 1
            while bit < chunks:
                if j & bit:
                    part = swap_groups(part, bit, rank_rows)
                bit *= 2
            result = part if result is None else result + part
        results.append(result)
        offset += wide
    return results


def partial_kernel(rank_rows, paired, places, out_ref, in_ref, *refs):
    *array_refs, held_ref = refs
    blocks = [(array_refs[i], row) for i, row in places]
    half = first_half(paired)
    held_out, held_in = both_projections(
        out_ref, in_ref, half, blocks, rank_rows, paired
    )
    held_ref[0] = held_out
    held_ref[1] = held_in


def score_kernel(rank_rows, paired, places, norm_ref, spread_ref, held_ref, out_ref, in_ref, *refs):
    *array_refs, score_ref = refs
    blocks = [(array_refs[i], row) for i, row in places]
    half = 1 - first_half(paired)
    held_out, held_in = both_projections(
        out_ref, in_ref, half, blocks, rank_rows, paired
    )
    product = (held_ref[0] + held_out) * (held_ref[1] + held_in)
    me = lax.axis_index("seq")
    lanes = lax.broadcasted_iota(jnp.int32, (1, product.shape[1]), 1)
    source = lanes // rank_rows
    if paired:
        source = source ^ me
    query = (source * rank_rows) // RANK
    seqs, tok_cap = -(-spread_ref.shape[0] // 8) * 8, spread_ref.shape[1]
    which = lax.broadcasted_iota(jnp.int32, (seqs, product.shape[1]), 0)
    sums = jnp.zeros(which.shape, jnp.float32)
    for k in range(spread_ref.shape[0]):
        sums = jnp.where(which == k, jnp.sum(product * spread_ref[k], axis=0, keepdims=True), sums)
    diagonal = lax.broadcasted_iota(jnp.int32, (seqs, tok_cap), 0) == lax.broadcasted_iota(
        jnp.int32, (seqs, tok_cap), 1
    )
    scale = jnp.sqrt(norm_ref[...] + EPSILON)
    for q in range(score_ref.shape[0]):
        value = jnp.sum(jnp.where(query == q, sums, 0.0), axis=1, keepdims=True)
        row = jnp.sum(jnp.where(diagonal, value, 0.0), axis=0, keepdims=True) / scale
        score_ref[q : q + 1, :] = row[:, : score_ref.shape[1]]


def gather_blocks(both, own, devices, lengths, member_step, head_step, norm_step, partial_step):
    def swap(value, mask):
        return lax.ppermute(value, "seq", [(i, i ^ mask) for i in range(devices)])

    def across(value):
        return lax.ppermute(value, "grp", [(0, 1), (1, 0)])

    gate = lambda *values: lax.optimization_barrier(values)
    stack = lambda *values: jnp.concatenate(values, axis=0)
    z1, z2, y0, both_core = swap(own, 4), swap(own, 8), swap(both, 2), swap(both, 1)
    z1, both_core, own = gate(z1, both_core, own)
    x1, y1, z3 = across(z1), swap(z1, 2), swap(own, 12)
    z2, y1, y0, lengths = gate(z2, y1, y0, lengths)
    x_near, y2 = across(stack(z2, y1)), swap(z2, 2)
    member, spread = member_step(lengths, x1)
    z3, y2, member = gate(z3, y2, member)
    head = head_step(member)
    x3, y3 = across(z3), swap(z3, 2)
    early = stack(y0, z1, y1, z2, x1)
    early_core = swap(early, 1)
    y3, x_near, head, member = gate(y3, x_near, head, member)
    x_last, yx2 = across(y3), swap(x_near[:PACK], 2)
    norms = norm_step(member, head)
    middle = stack(y2, z3, y3, x_near)
    middle_core = swap(middle, 1)
    mine, other = {}, {}

    def place(group, core, places):
        for i, (held, b) in enumerate(places):
            held[b], held[b + 1] = (group, i * PACK), (core, i * PACK)

    place(both, both_core, ((mine, 0), (other, 0)))
    place(early, early_core, ((mine, 2), (other, 2), (mine, 4), (mine, 6), (mine, 8), (other, 4)))
    place(middle, middle_core, ((mine, 10), (mine, 12), (mine, 14), (other, 8), (other, 6)))
    partial = partial_step([mine[b] for b in range(devices)])
    x_last, partial, norms = gate(x_last, partial, norms)
    late = stack(x3, yx2, x_last)
    place(late, swap(late, 1), ((other, 12), (other, 10), (other, 14)))
    return [other[b] for b in range(devices)], norms, spread, partial


def refs_of(blocks):
    arrays, places = [], []
    for value, row in blocks:
        seen = [i for i, array in enumerate(arrays) if array is value]
        if not seen:
            arrays.append(value)
        places.append((seen[0] if seen else len(arrays) - 1, row))
    return arrays, tuple(places)


def local(out_grads, layer_inputs, factor_u, factor_v, seq_lengths):
    devices = lax.axis_size("seq")
    paired = devices == 16 and lax.axis_size("grp") == 2
    seq_dev = seq_lengths.shape[0] // devices
    rank_rows = factor_u.shape[0]
    chunks = PACK // rank_rows
    queries = rank_rows * devices // RANK
    tok_cap, width_out = out_grads.shape
    width_in = layer_inputs.shape[1]
    width = width_out + width_in
    vmem = pl.BlockSpec(memory_space=pltpu.VMEM)
    hbm = pl.BlockSpec(memory_space=pltpu.HBM)

    score_params = pltpu.CompilerParams(vmem_limit_bytes=SCORE_VMEM)
    half_width = width // (2 * chunks)
    seqs = -(-seq_dev // 8) * 8
    packed = pl.pallas_call(
        functools.partial(pack_kernel, chunks, paired),
        out_shape=[jax.ShapeDtypeStruct((2 * PACK, half_width), factor_u.dtype)]
        + [jax.ShapeDtypeStruct((PACK, half_width), factor_u.dtype)] * paired,
        in_specs=[vmem] * 2,
        out_specs=[vmem] * (1 + paired),
        compiler_params=score_params,
    )(factor_u, factor_v)

    frows = devices * rank_rows
    tiny = pl.CostEstimate(flops=1, bytes_accessed=1, transcendentals=0)

    def member_step(lengths, earlier):
        return pl.pallas_call(
            functools.partial(member_kernel, seq_dev),
            out_shape=[
                jax.ShapeDtypeStruct((seqs, tok_cap), jnp.float32),
                jax.ShapeDtypeStruct((seq_dev, tok_cap, frows), jnp.float32),
            ],
            in_specs=[hbm] + [vmem] * 1,
            out_specs=[vmem] * 2,
            scratch_shapes=[pltpu.SMEM(lengths.shape, lengths.dtype), pltpu.SemaphoreType.DMA],
            compiler_params=score_params,
            cost_estimate=tiny,
        )(lengths, earlier)

    def head_step(member):
        return pl.pallas_call(
            head_kernel,
            out_shape=jax.ShapeDtypeStruct((tok_cap, tok_cap), jnp.float32),
            in_specs=[vmem] * 2,
            out_specs=vmem,
            compiler_params=score_params,
            cost_estimate=tiny,
        )(member, layer_inputs)

    def norm_step(*known):
        return pl.pallas_call(
            norm_kernel,
            out_shape=jax.ShapeDtypeStruct((1, tok_cap), jnp.float32),
            in_specs=[vmem] * 4,
            out_specs=vmem,
            compiler_params=score_params,
            cost_estimate=tiny,
        )(*known, out_grads, layer_inputs)

    def partial_step(blocks):
        arrays, places = refs_of(blocks)
        return pl.pallas_call(
            functools.partial(partial_kernel, rank_rows, paired, places),
            out_shape=jax.ShapeDtypeStruct((2, tok_cap, frows), jnp.float32),
            in_specs=[vmem] * (2 + len(arrays)),
            out_specs=vmem,
            compiler_params=score_params,
            cost_estimate=tiny,
        )(out_grads, layer_inputs, *arrays)

    if paired:
        other, norms, spread, partial = gather_blocks(
            packed[0], packed[1], devices, seq_lengths, member_step, head_step, norm_step, partial_step
        )
    else:
        member, spread = member_step(seq_lengths, packed[0])
        norms = norm_step(member, head_step(member))
        gathered = lax.all_gather(packed[0], "seq", axis=0, tiled=True)
        partial = partial_step([(gathered, 2 * PACK * b) for b in range(devices)])
        other = [(gathered, 2 * PACK * b + PACK) for b in range(devices)]
    arrays, places = refs_of(other)
    return pl.pallas_call(
        functools.partial(score_kernel, rank_rows, paired, places),
        out_shape=jax.ShapeDtypeStruct((queries, seq_dev), jnp.float32),
        in_specs=[vmem] * (5 + len(arrays)),
        out_specs=vmem,
        compiler_params=score_params,
        cost_estimate=tiny,
    )(norms, spread, partial, out_grads, layer_inputs, *arrays)


def solution(mesh):
    in_specs = (
        P(("grp", "seq"), None),
        P(("grp", "seq"), None),
        P("seq", None),
        P("seq", None),
        P("grp"),
    )
    out_specs = P(None, ("grp", "seq"))
    return jax.shard_map(local, mesh=mesh, in_specs=in_specs, out_specs=out_specs, check_vma=False)
```

```python
import functools

import jax
import jax.numpy as jnp
from jax import lax
from jax.experimental import pallas as pl
from jax.experimental.pallas import tpu as pltpu
from jax.sharding import PartitionSpec as P

RANK = 32
EPSILON = 1e-06
PACK = 16
HEAD = 2048
SCORE_VMEM = 24 * 1024 * 1024

NT = (((1,), (1,)), ((), ()))


def inner_rows(left, right):
    return lax.dot_general(left, right, NT, preferred_element_type=jnp.float32)


def first_half(paired):
    return lax.axis_index("grp") % 2 if paired else 0


def turn(paired, chunks):
    return lax.axis_index("seq") % chunks if paired else 0


def pack_kernel(chunks, paired, u_ref, v_ref, both_ref, *own_refs):
    rank_rows = u_ref.shape[0]
    turned = lax.axis_index("seq") % chunks
    wide_u, wide_v = u_ref.shape[1] // (2 * chunks), v_ref.shape[1] // (2 * chunks)
    for side in range(2):
        half = first_half(paired) ^ side
        place = 0
        for ref, wide in ((u_ref, wide_u), (v_ref, wide_v)):
            rows = []
            for g in range(chunks):
                start = pl.multiple_of(((g ^ turned) * 2 + half) * wide, 128)
                rows.append(ref[:, pl.ds(start, wide)].astype(jnp.float32))
            piece = jnp.concatenate(rows, axis=0).astype(both_ref.dtype)
            both_ref[side * PACK : (side + 1) * PACK, place : place + wide] = piece
            if side == 0:
                for own_ref in own_refs:
                    own_ref[:, place : place + wide] = piece
            place += wide


def member_kernel(seq_dev, lengths_hbm, after_ref, member_ref, spread_ref, lengths_ref, sem):
    copy = pltpu.make_async_copy(lengths_hbm, lengths_ref, sem)
    copy.start()
    copy.wait()
    seqs, tok_cap = member_ref.shape
    which = lax.broadcasted_iota(jnp.int32, (seqs, tok_cap), 0)
    position = lax.broadcasted_iota(jnp.int32, (seqs, tok_cap), 1)
    member = jnp.zeros((seqs, tok_cap), jnp.float32)
    rows = lax.broadcasted_iota(jnp.int32, spread_ref.shape[1:], 0)
    low = 0
    for k in range(seq_dev):
        high = low + lengths_ref[lax.axis_index("seq") * seq_dev + k]
        inside = (which == k) & (position >= low) & (position < high)
        member = jnp.where(inside, 1.0, member)
        spread_ref[k] = ((rows >= low) & (rows < high)).astype(jnp.float32)
        low = high
    member_ref[...] = member


def head_kernel(member_ref, in_ref, gram_ref):
    head = in_ref[:, :HEAD]
    gram_ref[...] = inner_rows(head, head)


def norm_kernel(member_ref, head_ref, out_ref, in_ref, norm_ref):
    tail = in_ref[:, HEAD:]
    paired = inner_rows(out_ref[...], out_ref[...]) * (head_ref[...] + inner_rows(tail, tail))
    member = member_ref[...]
    which = lax.broadcasted_iota(jnp.int32, member.shape, 0)
    position = lax.broadcasted_iota(jnp.int32, member.shape, 1)
    sums = jnp.dot(
        member, paired, precision=lax.Precision.HIGHEST, preferred_element_type=jnp.float32
    )
    value = jnp.sum(sums * member, axis=1, keepdims=True) / (out_ref.shape[1] * in_ref.shape[1])
    norm_ref[...] = jnp.sum(jnp.where(which == position, value, 0.0), axis=0, keepdims=True)


def swap_groups(value, bit, rank_rows):
    lanes = lax.broadcasted_iota(jnp.int32, (1, value.shape[1]), 1)
    shift = bit * rank_rows
    up = pltpu.roll(value, shift, 1)
    down = pltpu.roll(value, value.shape[1] - shift, 1)
    return jnp.where((lanes // shift) % 2 == 0, down, up)


def merged_rows(blocks, offset, wide, j, chunks, rank_rows):
    group = lax.broadcasted_iota(jnp.int32, (PACK, wide), 0) // rank_rows
    rows = []
    for first in range(0, len(blocks), chunks):
        merged = None
        for g in range(chunks):
            ref, row = blocks[first + (g ^ j)]
            piece = ref[row : row + PACK, offset : offset + wide]
            merged = piece if merged is None else jnp.where(group == g, piece, merged)
        rows.append(merged)
    return jnp.concatenate(rows, axis=0)


def both_projections(out_ref, in_ref, half, blocks, rank_rows, paired):
    chunks = PACK // rank_rows
    results, offset = [], 0
    for ref in (out_ref, in_ref):
        wide = ref.shape[1] // (2 * chunks)
        result = None
        for j in reversed(range(chunks)):
            rows = merged_rows(blocks, offset, wide, j, chunks, rank_rows)
            start = pl.multiple_of(((j ^ turn(paired, chunks)) * 2 + half) * wide, 128)
            part = inner_rows(ref[:, pl.ds(start, wide)], rows)
            bit = 1
            while bit < chunks:
                if j & bit:
                    part = swap_groups(part, bit, rank_rows)
                bit *= 2
            result = part if result is None else result + part
        results.append(result)
        offset += wide
    return results


def partial_kernel(rank_rows, paired, places, out_ref, in_ref, *refs):
    *array_refs, held_ref = refs
    blocks = [(array_refs[i], row) for i, row in places]
    half = first_half(paired)
    held_out, held_in = both_projections(
        out_ref, in_ref, half, blocks, rank_rows, paired
    )
    held_ref[0] = held_out
    held_ref[1] = held_in


def score_kernel(rank_rows, paired, places, norm_ref, spread_ref, held_ref, out_ref, in_ref, *refs):
    *array_refs, score_ref = refs
    blocks = [(array_refs[i], row) for i, row in places]
    half = 1 - first_half(paired)
    held_out, held_in = both_projections(
        out_ref, in_ref, half, blocks, rank_rows, paired
    )
    product = (held_ref[0] + held_out) * (held_ref[1] + held_in)
    me = lax.axis_index("seq")
    lanes = lax.broadcasted_iota(jnp.int32, (1, product.shape[1]), 1)
    source = lanes // rank_rows
    if paired:
        source = source ^ me
    query = (source * rank_rows) // RANK
    seqs, tok_cap = -(-spread_ref.shape[0] // 8) * 8, spread_ref.shape[1]
    which = lax.broadcasted_iota(jnp.int32, (seqs, product.shape[1]), 0)
    sums = jnp.zeros(which.shape, jnp.float32)
    for k in range(spread_ref.shape[0]):
        sums = jnp.where(which == k, jnp.sum(product * spread_ref[k], axis=0, keepdims=True), sums)
    diagonal = lax.broadcasted_iota(jnp.int32, (seqs, tok_cap), 0) == lax.broadcasted_iota(
        jnp.int32, (seqs, tok_cap), 1
    )
    scale = jnp.sqrt(norm_ref[...] + EPSILON)
    for q in range(score_ref.shape[0]):
        value = jnp.sum(jnp.where(query == q, sums, 0.0), axis=1, keepdims=True)
        row = jnp.sum(jnp.where(diagonal, value, 0.0), axis=0, keepdims=True) / scale
        score_ref[q : q + 1, :] = row[:, : score_ref.shape[1]]


def gather_blocks(both, own, devices, lengths, member_step, head_step, norm_step, partial_step):
    def swap(value, mask):
        return lax.ppermute(value, "seq", [(i, i ^ mask) for i in range(devices)])

    def across(value):
        return lax.ppermute(value, "grp", [(0, 1), (1, 0)])

    gate = lambda *values: lax.optimization_barrier(values)
    stack = lambda *values: jnp.concatenate(values, axis=0)
    z1, z2, y0, both_core = swap(own, 4), swap(own, 8), swap(both, 2), swap(both, 1)
    z1, both_core, own = gate(z1, both_core, own)
    x1, y1, z3 = across(z1), swap(z1, 2), swap(own, 12)
    z2, y1, y0, lengths = gate(z2, y1, y0, lengths)
    x_near, y2 = across(stack(z2, y1)), swap(z2, 2)
    member, spread = member_step(lengths, x1)
    z3, y2, member = gate(z3, y2, member)
    head = head_step(member)
    x3, y3 = across(z3), swap(z3, 2)
    early = stack(y0, z1, y1, z2, x1)
    early_core = swap(early, 1)
    y3, x_near, head, member = gate(y3, x_near, head, member)
    x_last, yx2 = across(y3), swap(x_near[:PACK], 2)
    norms = norm_step(member, head)
    middle = stack(y2, z3, y3, x_near)
    middle_core = swap(middle, 1)
    mine, other = {}, {}

    def place(group, core, places):
        for i, (held, b) in enumerate(places):
            held[b], held[b + 1] = (group, i * PACK), (core, i * PACK)

    place(both, both_core, ((mine, 0), (other, 0)))
    place(early, early_core, ((mine, 2), (other, 2), (mine, 4), (mine, 6), (mine, 8), (other, 4)))
    place(middle, middle_core, ((mine, 10), (mine, 12), (mine, 14), (other, 8), (other, 6)))
    partial = partial_step([mine[b] for b in range(devices)])
    x_last, partial, norms = gate(x_last, partial, norms)
    late = stack(x3, yx2, x_last)
    place(late, swap(late, 1), ((other, 12), (other, 10), (other, 14)))
    return [other[b] for b in range(devices)], norms, spread, partial


def refs_of(blocks):
    arrays, places = [], []
    for value, row in blocks:
        seen = [i for i, array in enumerate(arrays) if array is value]
        if not seen:
            arrays.append(value)
        places.append((seen[0] if seen else len(arrays) - 1, row))
    return arrays, tuple(places)


def local(out_grads, layer_inputs, factor_u, factor_v, seq_lengths):
    devices = lax.axis_size("seq")
    paired = devices == 16 and lax.axis_size("grp") == 2
    seq_dev = seq_lengths.shape[0] // devices
    rank_rows = factor_u.shape[0]
    chunks = PACK // rank_rows
    queries = rank_rows * devices // RANK
    tok_cap, width_out = out_grads.shape
    width_in = layer_inputs.shape[1]
    width = width_out + width_in
    vmem = pl.BlockSpec(memory_space=pltpu.VMEM)
    hbm = pl.BlockSpec(memory_space=pltpu.HBM)

    score_params = pltpu.CompilerParams(vmem_limit_bytes=SCORE_VMEM)
    half_width = width // (2 * chunks)
    seqs = -(-seq_dev // 8) * 8
    packed = pl.pallas_call(
        functools.partial(pack_kernel, chunks, paired),
        out_shape=[jax.ShapeDtypeStruct((2 * PACK, half_width), factor_u.dtype)]
        + [jax.ShapeDtypeStruct((PACK, half_width), factor_u.dtype)] * paired,
        in_specs=[vmem] * 2,
        out_specs=[vmem] * (1 + paired),
        compiler_params=score_params,
    )(factor_u, factor_v)

    frows = devices * rank_rows
    tiny = pl.CostEstimate(flops=1, bytes_accessed=1, transcendentals=0)

    def member_step(lengths, earlier):
        return pl.pallas_call(
            functools.partial(member_kernel, seq_dev),
            out_shape=[
                jax.ShapeDtypeStruct((seqs, tok_cap), jnp.float32),
                jax.ShapeDtypeStruct((seq_dev, tok_cap, frows), jnp.float32),
            ],
            in_specs=[hbm] + [vmem] * 1,
            out_specs=[vmem] * 2,
            scratch_shapes=[pltpu.SMEM(lengths.shape, lengths.dtype), pltpu.SemaphoreType.DMA],
            compiler_params=score_params,
            cost_estimate=tiny,
        )(lengths, earlier)

    def head_step(member):
        return pl.pallas_call(
            head_kernel,
            out_shape=jax.ShapeDtypeStruct((tok_cap, tok_cap), jnp.float32),
            in_specs=[vmem] * 2,
            out_specs=vmem,
            compiler_params=score_params,
            cost_estimate=tiny,
        )(member, layer_inputs)

    def norm_step(*known):
        return pl.pallas_call(
            norm_kernel,
            out_shape=jax.ShapeDtypeStruct((1, tok_cap), jnp.float32),
            in_specs=[vmem] * 4,
            out_specs=vmem,
            compiler_params=score_params,
            cost_estimate=tiny,
        )(*known, out_grads, layer_inputs)

    def partial_step(blocks):
        arrays, places = refs_of(blocks)
        return pl.pallas_call(
            functools.partial(partial_kernel, rank_rows, paired, places),
            out_shape=jax.ShapeDtypeStruct((2, tok_cap, frows), jnp.float32),
            in_specs=[vmem] * (2 + len(arrays)),
            out_specs=vmem,
            compiler_params=score_params,
            cost_estimate=tiny,
        )(out_grads, layer_inputs, *arrays)

    if paired:
        other, norms, spread, partial = gather_blocks(
            packed[0], packed[1], devices, seq_lengths, member_step, head_step, norm_step, partial_step
        )
    else:
        member, spread = member_step(seq_lengths, packed[0])
        norms = norm_step(member, head_step(member))
        gathered = lax.all_gather(packed[0], "seq", axis=0, tiled=True)
        partial = partial_step([(gathered, 2 * PACK * b) for b in range(devices)])
        other = [(gathered, 2 * PACK * b + PACK) for b in range(devices)]
    arrays, places = refs_of(other)
    return pl.pallas_call(
        functools.partial(score_kernel, rank_rows, paired, places),
        out_shape=jax.ShapeDtypeStruct((queries, seq_dev), jnp.float32),
        in_specs=[vmem] * (5 + len(arrays)),
        out_specs=vmem,
        compiler_params=score_params,
        cost_estimate=tiny,
    )(norms, spread, partial, out_grads, layer_inputs, *arrays)


def solution(mesh):
    in_specs = (
        P(("grp", "seq"), None),
        P(("grp", "seq"), None),
        P("seq", None),
        P("seq", None),
        P("grp"),
    )
    out_specs = P(None, ("grp", "seq"))
    return jax.shard_map(local, mesh=mesh, in_specs=in_specs, out_specs=out_specs, check_vma=False)
```

```python
import functools

import jax
import jax.numpy as jnp
from jax import lax
from jax.experimental import pallas as pl
from jax.experimental.pallas import tpu as pltpu
from jax.sharding import PartitionSpec as P

RANK = 32
EPSILON = 1e-06
PACK = 16
HEAD = 2048
SCORE_VMEM = 24 * 1024 * 1024

NT = (((1,), (1,)), ((), ()))


def inner_rows(left, right):
    return lax.dot_general(left, right, NT, preferred_element_type=jnp.float32)


def first_half(paired):
    return lax.axis_index("grp") % 2 if paired else 0


def turn(paired, chunks):
    return lax.axis_index("seq") % chunks if paired else 0


def pack_kernel(chunks, paired, u_ref, v_ref, both_ref, *own_refs):
    rank_rows = u_ref.shape[0]
    turned = lax.axis_index("seq") % chunks
    wide_u, wide_v = u_ref.shape[1] // (2 * chunks), v_ref.shape[1] // (2 * chunks)
    for side in range(2):
        half = first_half(paired) ^ side
        place = 0
        for ref, wide in ((u_ref, wide_u), (v_ref, wide_v)):
            rows = []
            for g in range(chunks):
                start = pl.multiple_of(((g ^ turned) * 2 + half) * wide, 128)
                rows.append(ref[:, pl.ds(start, wide)].astype(jnp.float32))
            piece = jnp.concatenate(rows, axis=0).astype(both_ref.dtype)
            both_ref[side * PACK : (side + 1) * PACK, place : place + wide] = piece
            if side == 0:
                for own_ref in own_refs:
                    own_ref[:, place : place + wide] = piece
            place += wide


def member_kernel(seq_dev, lengths_hbm, after_ref, member_ref, spread_ref, lengths_ref, sem):
    copy = pltpu.make_async_copy(lengths_hbm, lengths_ref, sem)
    copy.start()
    copy.wait()
    seqs, tok_cap = member_ref.shape
    which = lax.broadcasted_iota(jnp.int32, (seqs, tok_cap), 0)
    position = lax.broadcasted_iota(jnp.int32, (seqs, tok_cap), 1)
    member = jnp.zeros((seqs, tok_cap), jnp.float32)
    rows = lax.broadcasted_iota(jnp.int32, spread_ref.shape[1:], 0)
    low = 0
    for k in range(seq_dev):
        high = low + lengths_ref[lax.axis_index("seq") * seq_dev + k]
        inside = (which == k) & (position >= low) & (position < high)
        member = jnp.where(inside, 1.0, member)
        spread_ref[k] = ((rows >= low) & (rows < high)).astype(jnp.float32)
        low = high
    member_ref[...] = member


def head_kernel(member_ref, in_ref, gram_ref):
    head = in_ref[:, :HEAD]
    gram_ref[...] = inner_rows(head, head)


def norm_kernel(member_ref, head_ref, out_ref, in_ref, norm_ref):
    tail = in_ref[:, HEAD:]
    paired = inner_rows(out_ref[...], out_ref[...]) * (head_ref[...] + inner_rows(tail, tail))
    member = member_ref[...]
    which = lax.broadcasted_iota(jnp.int32, member.shape, 0)
    position = lax.broadcasted_iota(jnp.int32, member.shape, 1)
    sums = jnp.dot(
        member, paired, precision=lax.Precision.HIGHEST, preferred_element_type=jnp.float32
    )
    value = jnp.sum(sums * member, axis=1, keepdims=True) / (out_ref.shape[1] * in_ref.shape[1])
    norm_ref[...] = jnp.sum(jnp.where(which == position, value, 0.0), axis=0, keepdims=True)


def swap_groups(value, bit, rank_rows):
    lanes = lax.broadcasted_iota(jnp.int32, (1, value.shape[1]), 1)
    shift = bit * rank_rows
    up = pltpu.roll(value, shift, 1)
    down = pltpu.roll(value, value.shape[1] - shift, 1)
    return jnp.where((lanes // shift) % 2 == 0, down, up)


def merged_rows(blocks, offset, wide, j, chunks, rank_rows):
    group = lax.broadcasted_iota(jnp.int32, (PACK, wide), 0) // rank_rows
    rows = []
    for first in range(0, len(blocks), chunks):
        merged = None
        for g in range(chunks):
            ref, row = blocks[first + (g ^ j)]
            piece = ref[row : row + PACK, offset : offset + wide]
            merged = piece if merged is None else jnp.where(group == g, piece, merged)
        rows.append(merged)
    return jnp.concatenate(rows, axis=0)


def both_projections(out_ref, in_ref, half, blocks, rank_rows, paired):
    chunks = PACK // rank_rows
    results, offset = [], 0
    for ref in (out_ref, in_ref):
        wide = ref.shape[1] // (2 * chunks)
        result = None
        for j in reversed(range(chunks)):
            rows = merged_rows(blocks, offset, wide, j, chunks, rank_rows)
            start = pl.multiple_of(((j ^ turn(paired, chunks)) * 2 + half) * wide, 128)
            part = inner_rows(ref[:, pl.ds(start, wide)], rows)
            bit = 1
            while bit < chunks:
                if j & bit:
                    part = swap_groups(part, bit, rank_rows)
                bit *= 2
            result = part if result is None else result + part
        results.append(result)
        offset += wide
    return results


def partial_kernel(rank_rows, paired, places, out_ref, in_ref, *refs):
    *array_refs, held_ref = refs
    blocks = [(array_refs[i], row) for i, row in places]
    half = first_half(paired)
    held_out, held_in = both_projections(
        out_ref, in_ref, half, blocks, rank_rows, paired
    )
    held_ref[0] = held_out
    held_ref[1] = held_in


def score_kernel(rank_rows, paired, places, norm_ref, spread_ref, held_ref, out_ref, in_ref, *refs):
    *array_refs, score_ref = refs
    blocks = [(array_refs[i], row) for i, row in places]
    half = 1 - first_half(paired)
    held_out, held_in = both_projections(
        out_ref, in_ref, half, blocks, rank_rows, paired
    )
    product = (held_ref[0] + held_out) * (held_ref[1] + held_in)
    me = lax.axis_index("seq")
    lanes = lax.broadcasted_iota(jnp.int32, (1, product.shape[1]), 1)
    source = lanes // rank_rows
    if paired:
        source = source ^ me
    query = (source * rank_rows) // RANK
    seqs, tok_cap = -(-spread_ref.shape[0] // 8) * 8, spread_ref.shape[1]
    which = lax.broadcasted_iota(jnp.int32, (seqs, product.shape[1]), 0)
    sums = jnp.zeros(which.shape, jnp.float32)
    for k in range(spread_ref.shape[0]):
        sums = jnp.where(which == k, jnp.sum(product * spread_ref[k], axis=0, keepdims=True), sums)
    diagonal = lax.broadcasted_iota(jnp.int32, (seqs, tok_cap), 0) == lax.broadcasted_iota(
        jnp.int32, (seqs, tok_cap), 1
    )
    scale = jnp.sqrt(norm_ref[...] + EPSILON)
    for q in range(score_ref.shape[0]):
        value = jnp.sum(jnp.where(query == q, sums, 0.0), axis=1, keepdims=True)
        row = jnp.sum(jnp.where(diagonal, value, 0.0), axis=0, keepdims=True) / scale
        score_ref[q : q + 1, :] = row[:, : score_ref.shape[1]]


def gather_blocks(both, own, devices, lengths, member_step, head_step, norm_step, partial_step):
    def swap(value, mask):
        return lax.ppermute(value, "seq", [(i, i ^ mask) for i in range(devices)])

    def across(value):
        return lax.ppermute(value, "grp", [(0, 1), (1, 0)])

    gate = lambda *values: lax.optimization_barrier(values)
    stack = lambda *values: jnp.concatenate(values, axis=0)
    z1, z2, y0, both_core = swap(own, 4), swap(own, 8), swap(both, 2), swap(both, 1)
    z1, both_core, own = gate(z1, both_core, own)
    x1, y1, z3 = across(z1), swap(z1, 2), swap(own, 12)
    z2, y1, y0, lengths = gate(z2, y1, y0, lengths)
    x_near, y2 = across(stack(z2, y1)), swap(z2, 2)
    member, spread = member_step(lengths, x1)
    z3, y2, member = gate(z3, y2, member)
    head = head_step(member)
    y3 = swap(z3, 2)
    x3 = across(lax.optimization_barrier((z3, x1))[0])
    early = stack(y0, z1, y1, z2, x1)
    early_core = swap(early, 1)
    y3, x_near, head, member = gate(y3, x_near, head, member)
    x_last, yx2 = across(y3), swap(x_near[:PACK], 2)
    norms = norm_step(member, head)
    middle = stack(y2, z3, y3, x_near)
    middle_core = swap(middle, 1)
    mine, other = {}, {}

    def place(group, core, places):
        for i, (held, b) in enumerate(places):
            held[b], held[b + 1] = (group, i * PACK), (core, i * PACK)

    place(both, both_core, ((mine, 0), (other, 0)))
    place(early, early_core, ((mine, 2), (other, 2), (mine, 4), (mine, 6), (mine, 8), (other, 4)))
    place(middle, middle_core, ((mine, 10), (mine, 12), (mine, 14), (other, 8), (other, 6)))
    partial = partial_step([mine[b] for b in range(devices)])
    x_last, partial, norms = gate(x_last, partial, norms)
    late = stack(x3, yx2, x_last)
    place(late, swap(late, 1), ((other, 12), (other, 10), (other, 14)))
    return [other[b] for b in range(devices)], norms, spread, partial


def refs_of(blocks):
    arrays, places = [], []
    for value, row in blocks:
        seen = [i for i, array in enumerate(arrays) if array is value]
        if not seen:
            arrays.append(value)
        places.append((seen[0] if seen else len(arrays) - 1, row))
    return arrays, tuple(places)


def local(out_grads, layer_inputs, factor_u, factor_v, seq_lengths):
    devices = lax.axis_size("seq")
    paired = devices == 16 and lax.axis_size("grp") == 2
    seq_dev = seq_lengths.shape[0] // devices
    rank_rows = factor_u.shape[0]
    chunks = PACK // rank_rows
    queries = rank_rows * devices // RANK
    tok_cap, width_out = out_grads.shape
    width_in = layer_inputs.shape[1]
    width = width_out + width_in
    vmem = pl.BlockSpec(memory_space=pltpu.VMEM)
    hbm = pl.BlockSpec(memory_space=pltpu.HBM)

    score_params = pltpu.CompilerParams(vmem_limit_bytes=SCORE_VMEM)
    half_width = width // (2 * chunks)
    seqs = -(-seq_dev // 8) * 8
    packed = pl.pallas_call(
        functools.partial(pack_kernel, chunks, paired),
        out_shape=[jax.ShapeDtypeStruct((2 * PACK, half_width), factor_u.dtype)]
        + [jax.ShapeDtypeStruct((PACK, half_width), factor_u.dtype)] * paired,
        in_specs=[vmem] * 2,
        out_specs=[vmem] * (1 + paired),
        compiler_params=score_params,
    )(factor_u, factor_v)

    frows = devices * rank_rows
    tiny = pl.CostEstimate(flops=1, bytes_accessed=1, transcendentals=0)

    def member_step(lengths, earlier):
        return pl.pallas_call(
            functools.partial(member_kernel, seq_dev),
            out_shape=[
                jax.ShapeDtypeStruct((seqs, tok_cap), jnp.float32),
                jax.ShapeDtypeStruct((seq_dev, tok_cap, frows), jnp.float32),
            ],
            in_specs=[hbm] + [vmem] * 1,
            out_specs=[vmem] * 2,
            scratch_shapes=[pltpu.SMEM(lengths.shape, lengths.dtype), pltpu.SemaphoreType.DMA],
            compiler_params=score_params,
            cost_estimate=tiny,
        )(lengths, earlier)

    def head_step(member):
        return pl.pallas_call(
            head_kernel,
            out_shape=jax.ShapeDtypeStruct((tok_cap, tok_cap), jnp.float32),
            in_specs=[vmem] * 2,
            out_specs=vmem,
            compiler_params=score_params,
            cost_estimate=tiny,
        )(member, layer_inputs)

    def norm_step(*known):
        return pl.pallas_call(
            norm_kernel,
            out_shape=jax.ShapeDtypeStruct((1, tok_cap), jnp.float32),
            in_specs=[vmem] * 4,
            out_specs=vmem,
            compiler_params=score_params,
            cost_estimate=tiny,
        )(*known, out_grads, layer_inputs)

    def partial_step(blocks):
        arrays, places = refs_of(blocks)
        return pl.pallas_call(
            functools.partial(partial_kernel, rank_rows, paired, places),
            out_shape=jax.ShapeDtypeStruct((2, tok_cap, frows), jnp.float32),
            in_specs=[vmem] * (2 + len(arrays)),
            out_specs=vmem,
            compiler_params=score_params,
            cost_estimate=tiny,
        )(out_grads, layer_inputs, *arrays)

    if paired:
        other, norms, spread, partial = gather_blocks(
            packed[0], packed[1], devices, seq_lengths, member_step, head_step, norm_step, partial_step
        )
    else:
        member, spread = member_step(seq_lengths, packed[0])
        norms = norm_step(member, head_step(member))
        gathered = lax.all_gather(packed[0], "seq", axis=0, tiled=True)
        partial = partial_step([(gathered, 2 * PACK * b) for b in range(devices)])
        other = [(gathered, 2 * PACK * b + PACK) for b in range(devices)]
    arrays, places = refs_of(other)
    return pl.pallas_call(
        functools.partial(score_kernel, rank_rows, paired, places),
        out_shape=jax.ShapeDtypeStruct((queries, seq_dev), jnp.float32),
        in_specs=[vmem] * (5 + len(arrays)),
        out_specs=vmem,
        compiler_params=score_params,
        cost_estimate=tiny,
    )(norms, spread, partial, out_grads, layer_inputs, *arrays)


def solution(mesh):
    in_specs = (
        P(("grp", "seq"), None),
        P(("grp", "seq"), None),
        P("seq", None),
        P("seq", None),
        P("grp"),
    )
    out_specs = P(None, ("grp", "seq"))
    return jax.shard_map(local, mesh=mesh, in_specs=in_specs, out_specs=out_specs, check_vma=False)
```
